256 devices in a mesh: replica: 8 (over z), mp: 32 (over y, x, core).
Axes of the slice: x: 4, y: 4, z: 8, core: 2. Of those that a mesh axis runs over, the one named last changes fastest.
Arguments:
- partials: bfloat16 [8, 16, 512, 8192], P('replica', None, 'mp'), may hold values from -6 to 6
- owners: int32 [8, 16, 2], replicated, may hold values from 0 to 31, as said below
- step_count: int32 [], replicated, may hold values from 9000 to 9499
- basis_left: bfloat16 [8, 32, 2, 512, 512], P('replica', 'mp'), may hold values from -0.25 to 0.25
- basis_right: bfloat16 [8, 32, 2, 512, 512], P('replica', 'mp'), may hold values from -0.25 to 0.25
- moment_first: bfloat16 [8, 32, 2, 512, 512], P('replica', 'mp'), may hold values from -2 to 2
- moment_second: float32 [8, 32, 2, 512, 512], P('replica', 'mp'), may hold values from 1 to 10
Outputs:
- update: bfloat16 [16, 512, 8192], P(None, 'mp', 'replica')
- first_out: bfloat16 [8, 32, 2, 512, 512], P('replica', 'mp')
- second_out: float32 [8, 32, 2, 512, 512], P('replica', 'mp')
The draws below stay inside these ranges and needn't reach their ends.
Inputs may be any that keep to these rules, and one draw needn't show every extreme that they name: `owners`: for each replica index, every mp index owns at most 2 of its 32 tiles, and some mp index owns exactly 2.
All inputs are finite; a program needn't handle non-finite values.
Results may differ from the reference program's by a relative error of at most 0.022.
Values may be sent and summed in bfloat16 or wider, within the bound.
No kernel may reach another device: no remote copies, remote signals or barrier semaphores. Data moves between devices by JAX's collectives and lax.ppermute only.
A program may use at most 128 MiB of HBM per device.

```python
import math
import jax
import jax.numpy as jnp
from jax import lax

D = 8192
BLK = 512
CAP = 2
TILE_ROWS = 16
TCOLS = 2
N_REPLICA = 8
N_MP = 32


def owner_group(key):
    key_full, key_rest, key_reorder = jax.random.split(key, 3)
    fullest = jax.random.randint(key_full, (), 0, N_MP).astype(jnp.int32)
    spare_slots = N_MP * CAP - CAP
    shuffled = jax.random.permutation(key_rest, spare_slots)[:N_MP * CAP // 2 - CAP].astype(jnp.int32)
    shifted = shuffled + CAP * (shuffled >= CAP * fullest).astype(jnp.int32)
    owner_list = jnp.concatenate([jnp.full((CAP,), fullest, jnp.int32), (shifted // CAP).astype(jnp.int32)])
    reorder = jax.random.permutation(key_reorder, N_MP * CAP // 2)
    return owner_list[reorder]


def draw_owners(key, part):
    key = jax.random.fold_in(key, 11)
    group_keys = jax.random.split(key, N_REPLICA)
    groups = jax.vmap(owner_group)(group_keys)
    return groups.reshape(N_REPLICA, TILE_ROWS, TCOLS).astype(jnp.int32)


def strengthened(entries, key, source, target, blocks, factor):
    def block_of(dim):
        return (jnp.arange(entries.shape[dim]) // (entries.shape[dim] // blocks)).reshape((-1,) + (1,) * (entries.ndim - 1 - dim))

    near = jax.random.permutation(key, blocks)[block_of(target)]
    second = (block_of(target) + blocks // 2) % blocks
    return jnp.where((block_of(source) == near) | (block_of(source) == second), factor * entries, entries)


def level_of(stream_key, dims, pieces, smallest, largest):
    def one(axis_at, blocks):
        draws = jax.random.uniform(jax.random.fold_in(jax.random.fold_in(stream_key, 6), axis_at), (blocks,), jnp.float32, smallest / len(pieces), largest / len(pieces))
        return jnp.repeat(jnp.exp(draws), dims[axis_at] // blocks).reshape((-1,) + (1,) * (len(dims) - axis_at - 1))

    loudness = one(*pieces[0])
    for cut in pieces[1:]:
        loudness = loudness * one(*cut)
    return loudness


def normal_values(own_key, extent, scale, bound, cuts=(), kind=jnp.bfloat16):
    loudness = level_of(own_key, extent, cuts, -0.22, 0.18) if cuts else 1.0
    entries = jax.random.normal(own_key, extent, jnp.float32) * scale * loudness
    return jnp.minimum(jnp.maximum(entries, -bound), bound).astype(kind)


def heavy_noise(key, shape, width, bound, shards, heavy, kind=jnp.bfloat16):
    result = width * jax.random.normal(key, shape, jnp.float32)
    if shards:
        result = result * level_of(key, shape, shards, -0.22, 0.18)
    return jnp.clip(strengthened(result, jax.random.fold_in(key, 3), *heavy), -bound, bound).astype(kind)


def setup_inputs(seed: int = 0) -> dict:
    splits = jax.random.split(jax.random.key(seed), 8)
    return {
        "partials": heavy_noise(splits[0], (N_REPLICA, TILE_ROWS, BLK, D), 1.0, 6.0, ((0, 8), (2, 32)), (0, 3, 8, 2.0)),
        "owners": draw_owners(jax.random.fold_in(splits[7], 71), 0),
        "step_count": jax.random.randint(splits[2], (), 9000, 9500).astype(jnp.int32),
        "basis_left": normal_values(splits[3], (N_REPLICA, N_MP, CAP, BLK, BLK), BLK ** -0.5, 0.25, ((0, 8), (1, 32))),
        "basis_right": normal_values(splits[4], (N_REPLICA, N_MP, CAP, BLK, BLK), BLK ** -0.5, 0.25, ((0, 8), (1, 32))),
        "moment_first": normal_values(splits[5], (N_REPLICA, N_MP, CAP, BLK, BLK), 0.3, 2.0, ((0, 8), (1, 32))),
        "moment_second": jnp.clip(jnp.exp(math.log(10.0) - 2.3025851 * jax.random.uniform(splits[6], (N_REPLICA, N_MP, CAP, BLK, BLK), jnp.float32) ** level_of(splits[6], (N_REPLICA, N_MP, CAP, BLK, BLK), ((0, 8), (1, 32)), -0.2, 0.2)), 1.0, 10.0),
    }


beta_first = 0.9
beta_second = 0.95
epsilon = 1e-08
decay_start = 9000.0
decay_length = 1000.0

def slot_choice(owner_row, device_count, capacity):
    tile_count = owner_row.shape[0]
    positions = jnp.arange(tile_count, dtype=jnp.int32)
    earlier = (owner_row[:, None] == owner_row[None, :]) & (positions[None, :] < positions[:, None])
    ranked = lax.optimization_barrier(jnp.sum(earlier.astype(jnp.int32), axis=1)).astype(jnp.int32)
    devices = jnp.arange(device_count, dtype=jnp.int32)
    slot_ids = jnp.arange(capacity, dtype=jnp.int32)
    chosen = (owner_row[None, None, :] == devices[:, None, None]) & (ranked[None, None, :] == slot_ids[None, :, None])
    return (chosen, ranked)

def plan_terms(step_count):
    step_value = step_count.astype(jnp.float32)
    factor = 1.0 - (step_value - decay_start) / decay_length
    first_fix = 1.0 - jnp.power(jnp.float32(beta_first), step_value)
    second_fix = 1.0 - jnp.power(jnp.float32(beta_second), step_value)
    return (factor, first_fix, second_fix)

def soap_tiles(grad_tiles, basis_left, basis_right, moment_first, moment_second, factor, first_fix, second_fix):
    projected = jnp.einsum('...ab,...ac->...bc', basis_left.astype(jnp.float32), grad_tiles.astype(jnp.float32)).astype(jnp.bfloat16)
    rotated = jnp.einsum('...bc,...cd->...bd', projected.astype(jnp.float32), basis_right.astype(jnp.float32))
    first_new = beta_first * moment_first.astype(jnp.float32) + (1.0 - beta_first) * rotated
    second_new = beta_second * moment_second + (1.0 - beta_second) * rotated * rotated
    direction = (first_new / first_fix / (jnp.sqrt(second_new / second_fix) + epsilon)).astype(jnp.bfloat16)
    returned = jnp.einsum('...ab,...bc->...ac', basis_left.astype(jnp.float32), direction.astype(jnp.float32)).astype(jnp.bfloat16)
    update = jnp.einsum('...ac,...dc->...ad', returned.astype(jnp.float32), basis_right.astype(jnp.float32))
    return ((-factor * update).astype(jnp.bfloat16), first_new, second_new)

def reference(partials, owners, step_count, basis_left, basis_right, moment_first, moment_second):
    factor, first_fix, second_fix = plan_terms(step_count)
    total = jnp.zeros(partials.shape[1:], jnp.float32)
    for source_replica in range(N_REPLICA):
        total = total + partials[source_replica].astype(jnp.float32)
    grad_half = total.astype(jnp.bfloat16)
    block_width = TCOLS * BLK
    update_blocks = []
    first_groups = []
    second_groups = []
    for replica_id in range(N_REPLICA):
        column_block = grad_half[:, :, replica_id * block_width:(replica_id + 1) * block_width]
        group_tiles = column_block.reshape(TILE_ROWS, BLK, TCOLS, BLK).transpose(0, 2, 1, 3).reshape(TILE_ROWS * TCOLS, BLK, BLK)
        owner_row = owners[replica_id].reshape(-1).astype(jnp.int32)
        chosen, ranked = slot_choice(owner_row, N_MP, CAP)
        positions = jnp.arange(owner_row.shape[0], dtype=jnp.int32)
        tile_index = lax.optimization_barrier(jnp.sum(jnp.where(chosen, positions[None, None, :], 0), axis=2)).astype(jnp.int32)
        occupied = jnp.any(chosen, axis=2)
        slot_tiles = jnp.where(occupied[:, :, None, None], group_tiles[tile_index], jnp.zeros((), jnp.bfloat16))
        update, first_new, second_new = soap_tiles(slot_tiles, basis_left[replica_id], basis_right[replica_id], moment_first[replica_id], moment_second[replica_id], factor, first_fix, second_fix)
        first_groups.append(jnp.where(occupied[:, :, None, None], first_new.astype(jnp.bfloat16), moment_first[replica_id]))
        second_groups.append(jnp.where(occupied[:, :, None, None], second_new, moment_second[replica_id]))
        tile_updates = update[owner_row, ranked]
        update_blocks.append(tile_updates.reshape(TILE_ROWS, TCOLS, BLK, BLK).transpose(0, 2, 1, 3).reshape(TILE_ROWS, BLK, block_width))
    return (jnp.concatenate(update_blocks, axis=2), jnp.stack(first_groups), jnp.stack(second_groups))
```

```python
import functools
import jax
import jax.numpy as jnp
from jax import lax
from jax.experimental import pallas as pl
from jax.experimental.pallas import tpu as pltpu
from jax.sharding import PartitionSpec as P

bf16 = jnp.bfloat16
f32 = jnp.float32
beta_first = 0.9
beta_second = 0.95
epsilon = 1e-08
decay_start = 9000.0
decay_length = 1000.0
VMEM_LIMIT = 40 * 1024 * 1024


def plan_kernel(devices_mp, capacity, where_ref, owners_ref, tile_of_ref, slot_of_ref, held_ref):
    replica_id, my_index = where_ref[0], where_ref[1]
    tiles = slot_of_ref.shape[0]
    for i in range(devices_mp * capacity):
        tile_of_ref[i] = 0
    counts = tile_of_ref.shape[0] - devices_mp
    for m in range(devices_mp):
        tile_of_ref[counts + m] = 0

    def step(t, carry):
        owner = owners_ref[replica_id * tiles + t]
        rank = tile_of_ref[counts + owner]
        tile_of_ref[counts + owner] = rank + 1
        slot = owner * capacity + rank
        tile_of_ref[slot] = t
        slot_of_ref[t] = slot
        return carry

    lax.fori_loop(0, tiles, step, 0)
    held_ref[0] = tile_of_ref[counts + my_index]


def make_plan(owners, replica_id, my_index, devices_mp, capacity):
    tiles = owners.shape[1] * owners.shape[2]
    where = jnp.stack([replica_id, my_index]).astype(jnp.int32)
    smem = pl.BlockSpec(memory_space=pltpu.SMEM)
    return pl.pallas_call(
        functools.partial(plan_kernel, devices_mp, capacity),
        out_shape=(
            jax.ShapeDtypeStruct((devices_mp * (capacity + 1),), jnp.int32),
            jax.ShapeDtypeStruct((tiles,), jnp.int32),
            jax.ShapeDtypeStruct((1,), jnp.int32),
        ),
        in_specs=[smem, smem],
        out_specs=(smem, smem, smem),
        name="plan",
    )(where, owners.reshape(-1))


def pack_kernel(tile_of_ref, replica_ref, own_ref, left_ref, right_ref, out_ref, sums_ref):
    tile_rows, sub_rows, width = own_ref.shape
    half = width // 2
    for l in range(tile_rows):
        total = (
            own_ref[l].astype(f32) + left_ref[l].astype(f32) + right_ref[l].astype(f32)
        ).astype(bf16)
        sums_ref[2 * l] = total[:, :half]
        sums_ref[2 * l + 1] = total[:, half:]
    devices_mp, capacity = out_ref.shape[:2]

    def step(m, carry):
        for c in range(capacity):
            out_ref[m, c] = sums_ref[tile_of_ref[m * capacity + c]]
        return carry

    lax.fori_loop(0, devices_mp, step, 0, unroll=4)


def pack(tile_of, replica_id, part, left, right, devices_mp, capacity):
    tile_rows, sub_rows, width = left.shape
    whole = pl.BlockSpec((tile_rows, sub_rows, width), lambda i, *_: (0, 0, 0))
    shape = (devices_mp, capacity, sub_rows, width // 2)
    return pl.pallas_call(
        pack_kernel,
        grid_spec=pltpu.PrefetchScalarGridSpec(
            num_scalar_prefetch=2,
            grid=(1,),
            in_specs=[
                pl.BlockSpec(
                    (tile_rows, sub_rows, width), lambda i, tile_of, replica: (0, 0, replica[0])
                ),
                whole,
                whole,
            ],
            out_specs=pl.BlockSpec(shape, lambda i, *_: (0, 0, 0, 0)),
            scratch_shapes=[pltpu.VMEM((2 * tile_rows, sub_rows, width // 2), bf16)],
        ),
        out_shape=jax.ShapeDtypeStruct(shape, bf16),
        compiler_params=pltpu.CompilerParams(vmem_limit_bytes=VMEM_LIMIT),
        name="pack",
    )(tile_of, replica_id.reshape(1), part, left, right)


def dot(a, b):
    return jnp.dot(a, b, preferred_element_type=f32)


def tile_kernel(
    held_ref, terms_ref, grad_ref, left_t_ref, left_ref, right_ref, right_t_ref, first_ref, second_ref,
    update_ref, first_out_ref, second_out_ref,
):
    slot = pl.program_id(0)
    occupied = slot < held_ref[0]

    @pl.when(occupied)
    def _():
        devices_mp, _, sub_rows, size = grad_ref.shape
        grad = grad_ref[...].reshape(size, size)
        projected = dot(left_t_ref[0], grad).astype(bf16)
        rotated = dot(projected, right_ref[0])
        first_new = beta_first * first_ref[0].astype(f32) + (1.0 - beta_first) * rotated
        second_new = beta_second * second_ref[0] + (1.0 - beta_second) * rotated * rotated
        first_out_ref[0] = first_new.astype(bf16)
        second_out_ref[0] = second_new
        direction = (
            first_new / terms_ref[1] / (jnp.sqrt(second_new / terms_ref[2]) + epsilon)
        ).astype(bf16)
        returned = dot(left_ref[0], direction).astype(bf16)
        update = (terms_ref[0] * dot(returned, right_t_ref[0])).astype(bf16)
        update_ref[...] = update.reshape(update_ref.shape)

    @pl.when(jnp.logical_not(occupied))
    def _():
        first_out_ref[...] = first_ref[...]
        second_out_ref[...] = second_ref[...]
        update_ref[...] = jnp.zeros_like(update_ref)


def tile_update(held, terms, grads, left_t, left, right, right_t, first, second):
    devices_mp, capacity, sub_rows, size = grads.shape
    smem = pl.BlockSpec(memory_space=pltpu.SMEM)
    square = pl.BlockSpec((1, size, size), lambda s: (s, 0, 0))
    spread = pl.BlockSpec((devices_mp, 1, sub_rows, size), lambda s: (0, s, 0, 0))
    return pl.pallas_call(
        tile_kernel,
        grid=(capacity,),
        in_specs=[smem, smem, spread] + [square] * 6,
        out_specs=(spread, square, square),
        out_shape=(
            jax.ShapeDtypeStruct(grads.shape, bf16),
            jax.ShapeDtypeStruct(first.shape, bf16),
            jax.ShapeDtypeStruct(second.shape, f32),
        ),
        compiler_params=pltpu.CompilerParams(vmem_limit_bytes=VMEM_LIMIT),
        name="tile_update",
    )(held, terms, grads, left_t, left, right, right_t, first, second)


def place_kernel(slot_of_ref, back_ref, out_ref):
    tile_rows, sub_rows, width = out_ref.shape
    half = width // 2

    def step(l, carry):
        out_ref[l, :, :half] = back_ref[slot_of_ref[2 * l]]
        out_ref[l, :, half:] = back_ref[slot_of_ref[2 * l + 1]]
        return carry

    lax.fori_loop(0, tile_rows, step, 0, unroll=4)


def place(slot_of, back, tile_rows):
    slots, sub_rows, size = back.shape
    vmem = pl.BlockSpec(memory_space=pltpu.VMEM)
    return pl.pallas_call(
        place_kernel,
        in_specs=[pl.BlockSpec(memory_space=pltpu.SMEM), vmem],
        out_specs=vmem,
        out_shape=jax.ShapeDtypeStruct((tile_rows, sub_rows, 2 * size), bf16),
        compiler_params=pltpu.CompilerParams(vmem_limit_bytes=VMEM_LIMIT),
        name="place",
    )(slot_of, back)


def summed_ends(part, replica_id, replicas, width):
    tile_rows, sub_rows, _ = part.shape
    half = width // 2
    up = [(i, (i + 1) % replicas) for i in range(replicas)]
    down = [(i, (i - 1) % replicas) for i in range(replicas)]
    far = replicas // 2

    def block(offset, start, size):
        column = lax.rem(replica_id + offset + replicas, replicas) * width + start
        return lax.dynamic_slice(part, (0, 0, column), (tile_rows, sub_rows, size))

    def add(a, b):
        return (a.astype(f32) + b.astype(f32)).astype(bf16)

    from_above = lax.ppermute(block(far, 0, half), "replica", down)
    from_below = lax.ppermute(block(far, half, half), "replica", up)
    for hops in range(far - 1, 0, -1):
        low, high = block(-hops, 0, width), block(hops, 0, width)
        if hops == far - 1:
            low = jnp.concatenate([add(low[..., :half], from_above), low[..., half:]], axis=2)
            high = jnp.concatenate([high[..., :half], add(high[..., half:], from_below)], axis=2)
        else:
            low, high = add(low, from_above), add(high, from_below)
        low, high = lax.optimization_barrier((low, high))
        from_above = lax.ppermute(low, "replica", down)
        from_below = lax.ppermute(high, "replica", up)
    return from_above, from_below


def body(partials, owners, step_count, basis_left, basis_right, moment_first, moment_second):
    replicas = lax.axis_size("replica")
    devices_mp = lax.axis_size("mp")
    replica_id = lax.axis_index("replica").astype(jnp.int32)
    my_index = lax.axis_index("mp").astype(jnp.int32)
    part = partials[0]
    tile_rows, sub_rows, width = part.shape
    capacity = basis_left.shape[2]
    width = width // replicas
    tile_of, slot_of, held = make_plan(owners, replica_id, my_index, devices_mp, capacity)
    step_value = step_count.astype(f32)
    factor = 1.0 - (step_value - decay_start) / decay_length
    first_fix = 1.0 - jnp.power(f32(beta_first), step_value)
    second_fix = 1.0 - jnp.power(f32(beta_second), step_value)
    terms = jnp.stack([-factor, first_fix, second_fix])
    left, right = basis_left[0, 0], basis_right[0, 0]
    left_t, right_t = jnp.swapaxes(left, 1, 2), jnp.swapaxes(right, 1, 2)

    from_above, from_below = summed_ends(part, replica_id, replicas, width)
    outgoing = pack(tile_of, replica_id, part, from_above, from_below, devices_mp, capacity)
    arrived = lax.all_to_all(outgoing, "mp", split_axis=0, concat_axis=0, tiled=True)
    update, first_out, second_out = tile_update(
        held, terms, arrived, left_t, left, right, right_t, moment_first[0, 0], moment_second[0, 0]
    )
    back = lax.all_to_all(update, "mp", split_axis=0, concat_axis=0, tiled=True)
    slab = place(slot_of, back.reshape(devices_mp * capacity, sub_rows, width // 2), tile_rows)
    return slab, first_out[None, None], second_out[None, None]


def solution(mesh):
    in_specs = (
        P("replica", None, "mp", None),
        P(),
        P(),
        P("replica", "mp", None, None, None),
        P("replica", "mp", None, None, None),
        P("replica", "mp", None, None, None),
        P("replica", "mp", None, None, None),
    )
    out_specs = (
        P(None, "mp", "replica"),
        P("replica", "mp", None, None, None),
        P("replica", "mp", None, None, None),
    )
    return jax.shard_map(body, mesh=mesh, in_specs=in_specs, out_specs=out_specs, check_vma=False)
```

```python
import functools
import jax
import jax.numpy as jnp
from jax import lax
from jax.experimental import pallas as pl
from jax.experimental.pallas import tpu as pltpu
from jax.sharding import PartitionSpec as P

bf16 = jnp.bfloat16
f32 = jnp.float32
beta_first = 0.9
beta_second = 0.95
epsilon = 1e-08
decay_start = 9000.0
decay_length = 1000.0
VMEM_LIMIT = 40 * 1024 * 1024
TILE_VMEM = 60 * 1024 * 1024


def plan_kernel(devices_mp, capacity, where_ref, owners_ref, tile_of_ref, slot_of_ref, held_ref):
    replica_id, my_index = where_ref[0], where_ref[1]
    tiles = slot_of_ref.shape[0]
    for i in range(devices_mp * capacity):
        tile_of_ref[i] = 0
    counts = tile_of_ref.shape[0] - devices_mp
    for m in range(devices_mp):
        tile_of_ref[counts + m] = 0

    def step(t, carry):
        owner = owners_ref[replica_id * tiles + t]
        rank = tile_of_ref[counts + owner]
        tile_of_ref[counts + owner] = rank + 1
        slot = owner * capacity + rank
        tile_of_ref[slot] = t
        slot_of_ref[t] = slot
        return carry

    lax.fori_loop(0, tiles, step, 0)
    held_ref[0] = tile_of_ref[counts + my_index]


def make_plan(owners, replica_id, my_index, devices_mp, capacity):
    tiles = owners.shape[1] * owners.shape[2]
    where = jnp.stack([replica_id, my_index]).astype(jnp.int32)
    smem = pl.BlockSpec(memory_space=pltpu.SMEM)
    return pl.pallas_call(
        functools.partial(plan_kernel, devices_mp, capacity),
        out_shape=(
            jax.ShapeDtypeStruct((devices_mp * (capacity + 1),), jnp.int32),
            jax.ShapeDtypeStruct((tiles,), jnp.int32),
            jax.ShapeDtypeStruct((1,), jnp.int32),
        ),
        in_specs=[smem, smem],
        out_specs=(smem, smem, smem),
        name="plan",
    )(where, owners.reshape(-1))


def pack_kernel(tile_of_ref, own_ref, above_ref, below_ref, out_ref, sums_ref):
    tile_rows, sub_rows, width = own_ref.shape
    half = width // 2
    for l in range(tile_rows):
        total = (
            own_ref[l].astype(f32) + above_ref[l].astype(f32) + below_ref[l].astype(f32)
        ).astype(bf16)
        sums_ref[2 * l] = total[:, :half]
        sums_ref[2 * l + 1] = total[:, half:]
    devices_mp, capacity = out_ref.shape[:2]

    def step(m, carry):
        for c in range(capacity):
            out_ref[m, c] = sums_ref[tile_of_ref[m * capacity + c]]
        return carry

    lax.fori_loop(0, devices_mp, step, 0, unroll=4)


def pack(tile_of, own, above, below, devices_mp, capacity):
    tile_rows, sub_rows, width = own.shape
    vmem = pl.BlockSpec(memory_space=pltpu.VMEM)
    return pl.pallas_call(
        pack_kernel,
        in_specs=[pl.BlockSpec(memory_space=pltpu.SMEM), vmem, vmem, vmem],
        out_specs=vmem,
        out_shape=jax.ShapeDtypeStruct((devices_mp, capacity, sub_rows, width // 2), bf16),
        scratch_shapes=[pltpu.VMEM((2 * tile_rows, sub_rows, width // 2), bf16)],
        compiler_params=pltpu.CompilerParams(vmem_limit_bytes=VMEM_LIMIT),
        name="pack",
    )(tile_of, own, above, below)


def dot(a, b):
    return jnp.dot(a, b, preferred_element_type=f32)


def tile_kernel(
    held_ref, terms_ref, grad_hbm, left_t_hbm, left_hbm, right_hbm, right_t_hbm, first_hbm, second_hbm,
    update_hbm, first_out_hbm, second_out_hbm,
    grad, left_t, left, right, right_t, first, second, update, first_out, second_out, sems, out_sems,
):
    capacity, size, _ = left.shape
    operands = (
        (grad_hbm, grad), (left_t_hbm, left_t), (right_hbm, right), (second_hbm, second),
        (first_hbm, first), (left_hbm, left), (right_t_hbm, right_t),
    )

    def fetch(s):
        copies = []
        for k, (src, dst) in enumerate(operands):
            source = src.at[:, s] if k == 0 else src.at[s]
            copies.append(pltpu.make_async_copy(source, dst.at[s], sems.at[s, k]))
        return copies

    def drain(s):
        return [
            pltpu.make_async_copy(update.at[s], update_hbm.at[:, s], out_sems.at[s, 0]),
            pltpu.make_async_copy(first_out.at[s], first_out_hbm.at[s], out_sems.at[s, 1]),
            pltpu.make_async_copy(second_out.at[s], second_out_hbm.at[s], out_sems.at[s, 2]),
        ]

    arrivals = [fetch(s) for s in range(capacity)]
    for copies in arrivals:
        for copy in copies:
            copy.start()
    for s in range(capacity):
        copies, leaving = arrivals[s], drain(s)
        occupied = s < held_ref[0]

        @pl.when(occupied)
        def _():
            copies[0].wait()
            copies[1].wait()
            projected = dot(left_t[s], grad[s].reshape(size, size)).astype(bf16)
            copies[2].wait()
            rotated = dot(projected, right[s])
            copies[3].wait()
            copies[4].wait()
            first_new = beta_first * first[s].astype(f32) + (1.0 - beta_first) * rotated
            second_new = beta_second * second[s] + (1.0 - beta_second) * rotated * rotated
            first_out[s] = first_new.astype(bf16)
            second_out[s] = second_new
            direction = (
                first_new / terms_ref[1] / (jnp.sqrt(second_new / terms_ref[2]) + epsilon)
            ).astype(bf16)
            copies[5].wait()
            returned = dot(left[s], direction).astype(bf16)
            copies[6].wait()
            step = (terms_ref[0] * dot(returned, right_t[s])).astype(bf16)
            update[s] = step.reshape(update.shape[1:])

        @pl.when(jnp.logical_not(occupied))
        def _():
            for copy in copies:
                copy.wait()
            first_out[s] = first[s]
            second_out[s] = second[s]
            update[s] = jnp.zeros(update.shape[1:], bf16)

        for copy in leaving:
            copy.start()
    for s in range(capacity):
        for copy in drain(s):
            copy.wait()


def tile_update(held, terms, grads, left_t, left, right, right_t, first, second):
    devices_mp, capacity, sub_rows, size = grads.shape
    smem = pl.BlockSpec(memory_space=pltpu.SMEM)
    hbm = pl.BlockSpec(memory_space=pl.ANY)
    rows = pltpu.VMEM((capacity, devices_mp, sub_rows, size), bf16)
    square = pltpu.VMEM((capacity, size, size), bf16)
    wide = pltpu.VMEM((capacity, size, size), f32)
    return pl.pallas_call(
        tile_kernel,
        in_specs=[smem, smem] + [hbm] * 7,
        out_specs=(hbm, hbm, hbm),
        out_shape=(
            jax.ShapeDtypeStruct(grads.shape, bf16),
            jax.ShapeDtypeStruct(first.shape, bf16),
            jax.ShapeDtypeStruct(second.shape, f32),
        ),
        scratch_shapes=[
            rows, square, square, square, square, square, wide, rows, square, wide,
            pltpu.SemaphoreType.DMA((capacity, 7)),
            pltpu.SemaphoreType.DMA((capacity, 3)),
        ],
        compiler_params=pltpu.CompilerParams(vmem_limit_bytes=TILE_VMEM),
        name="tile_update",
    )(held, terms, grads, left_t, left, right, right_t, first, second)


def place_kernel(slot_of_ref, back_ref, out_ref):
    tile_rows, sub_rows, width = out_ref.shape
    half = width // 2

    def step(l, carry):
        out_ref[l, :, :half] = back_ref[slot_of_ref[2 * l]]
        out_ref[l, :, half:] = back_ref[slot_of_ref[2 * l + 1]]
        return carry

    lax.fori_loop(0, tile_rows, step, 0, unroll=4)


def place(slot_of, back, tile_rows):
    slots, sub_rows, size = back.shape
    vmem = pl.BlockSpec(memory_space=pltpu.VMEM)
    return pl.pallas_call(
        place_kernel,
        in_specs=[pl.BlockSpec(memory_space=pltpu.SMEM), vmem],
        out_specs=vmem,
        out_shape=jax.ShapeDtypeStruct((tile_rows, sub_rows, 2 * size), bf16),
        compiler_params=pltpu.CompilerParams(vmem_limit_bytes=VMEM_LIMIT),
        name="place",
    )(slot_of, back)


def summed_ends(part, replica_id, replicas, width, early):
    tile_rows, sub_rows, _ = part.shape
    half = width // 2
    up = [(i, (i + 1) % replicas) for i in range(replicas)]
    down = [(i, (i - 1) % replicas) for i in range(replicas)]
    far = replicas // 2

    def block(offset, start, size):
        column = lax.rem(replica_id + offset + replicas, replicas) * width + start
        return lax.dynamic_slice(part, (0, 0, column), (tile_rows, sub_rows, size))

    low, high = lax.optimization_barrier((block(far, 0, half), block(far, half, half)))
    from_above = lax.ppermute(low, "replica", down)
    from_below = lax.ppermute(high, "replica", up)
    for hops in range(far - 1, 0, -1):
        low, high = block(-hops, 0, width), block(hops, 0, width)
        if hops == far - 1:
            low = jnp.concatenate([low[..., :half] + from_above, low[..., half:]], axis=2)
            high = jnp.concatenate([high[..., :half], high[..., half:] + from_below], axis=2)
        else:
            low, high = low + from_above, high + from_below
        low, high, early = lax.optimization_barrier((low, high, early))
        from_above = lax.ppermute(low, "replica", down)
        from_below = lax.ppermute(high, "replica", up)
    own = block(0, 0, width)
    return own, from_above, from_below, early


def body(partials, owners, step_count, basis_left, basis_right, moment_first, moment_second):
    replicas = lax.axis_size("replica")
    devices_mp = lax.axis_size("mp")
    replica_id = lax.axis_index("replica").astype(jnp.int32)
    my_index = lax.axis_index("mp").astype(jnp.int32)
    part = partials[0]
    tile_rows, sub_rows, width = part.shape
    capacity = basis_left.shape[2]
    width = width // replicas
    tile_of, slot_of, held = make_plan(owners, replica_id, my_index, devices_mp, capacity)
    step_value = step_count.astype(f32)
    factor = 1.0 - (step_value - decay_start) / decay_length
    first_fix = 1.0 - jnp.power(f32(beta_first), step_value)
    second_fix = 1.0 - jnp.power(f32(beta_second), step_value)
    terms = jnp.stack([-factor, first_fix, second_fix])
    left, right = basis_left[0, 0], basis_right[0, 0]
    left_t, right_t = jnp.swapaxes(left, 1, 2), jnp.swapaxes(right, 1, 2)

    early = (tile_of, slot_of, held, terms, left_t, right_t)
    own, above, below, early = summed_ends(part, replica_id, replicas, width, early)
    tile_of, slot_of, held, terms, left_t, right_t = early
    outgoing = pack(tile_of, own, above, below, devices_mp, capacity)
    arrived = lax.all_to_all(outgoing, "mp", split_axis=0, concat_axis=0, tiled=True)
    update, first_out, second_out = tile_update(
        held, terms, arrived, left_t, left, right, right_t, moment_first[0, 0], moment_second[0, 0]
    )
    back = lax.all_to_all(update, "mp", split_axis=0, concat_axis=0, tiled=True)
    slab = place(slot_of, back.reshape(devices_mp * capacity, sub_rows, width // 2), tile_rows)
    return slab, first_out[None, None], second_out[None, None]


def solution(mesh):
    in_specs = (
        P("replica", None, "mp", None),
        P(),
        P(),
        P("replica", "mp", None, None, None),
        P("replica", "mp", None, None, None),
        P("replica", "mp", None, None, None),
        P("replica", "mp", None, None, None),
    )
    out_specs = (
        P(None, "mp", "replica"),
        P("replica", "mp", None, None, None),
        P("replica", "mp", None, None, None),
    )
    return jax.shard_map(body, mesh=mesh, in_specs=in_specs, out_specs=out_specs, check_vma=False)
```

```python
import functools
import jax
import jax.numpy as jnp
from jax import lax
from jax.experimental import pallas as pl
from jax.experimental.pallas import tpu as pltpu
from jax.sharding import PartitionSpec as P

bf16 = jnp.bfloat16
f32 = jnp.float32
beta_first = 0.9
beta_second = 0.95
epsilon = 1e-08
decay_start = 9000.0
decay_length = 1000.0
MIB = 1024 * 1024
VMEM_LIMIT = 16 * MIB
TILE_VMEM = 32 * MIB
SMALL_VMEM = 16 * MIB


def plan_kernel(devices_mp, capacity, where_ref, owners_ref, tile_of_ref, slot_of_ref, held_ref):
    replica_id, my_index = where_ref[0], where_ref[1]
    tiles = slot_of_ref.shape[0]
    for i in range(devices_mp * capacity):
        tile_of_ref[i] = 0
    counts = tile_of_ref.shape[0] - devices_mp
    for m in range(devices_mp):
        tile_of_ref[counts + m] = 0

    def step(t, carry):
        owner = owners_ref[replica_id * tiles + t]
        rank = tile_of_ref[counts + owner]
        tile_of_ref[counts + owner] = rank + 1
        slot = owner * capacity + rank
        tile_of_ref[slot] = t
        slot_of_ref[t] = slot
        return carry

    lax.fori_loop(0, tiles, step, 0)
    held_ref[0] = tile_of_ref[counts + my_index]


def make_plan(owners, replica_id, my_index, devices_mp, capacity):
    tiles = owners.shape[1] * owners.shape[2]
    where = jnp.stack([replica_id, my_index]).astype(jnp.int32)
    smem = pl.BlockSpec(memory_space=pltpu.SMEM)
    return pl.pallas_call(
        functools.partial(plan_kernel, devices_mp, capacity),
        out_shape=(
            jax.ShapeDtypeStruct((devices_mp * (capacity + 1),), jnp.int32),
            jax.ShapeDtypeStruct((tiles,), jnp.int32),
            jax.ShapeDtypeStruct((1,), jnp.int32),
        ),
        in_specs=[smem, smem],
        out_specs=(smem, smem, smem),
        name="plan",
    )(where, owners.reshape(-1))


def pack_kernel(tile_of_ref, own_ref, above_ref, below_ref, out_ref, sums_ref):
    tile_rows, sub_rows, width = own_ref.shape
    half = width // 2
    for l in range(tile_rows):
        total = (
            own_ref[l].astype(f32) + above_ref[l].astype(f32) + below_ref[l].astype(f32)
        ).astype(bf16)
        sums_ref[2 * l] = total[:, :half]
        sums_ref[2 * l + 1] = total[:, half:]
    devices_mp, capacity = out_ref.shape[:2]

    def step(m, carry):
        for c in range(capacity):
            out_ref[m, c] = sums_ref[tile_of_ref[m * capacity + c]]
        return carry

    lax.fori_loop(0, devices_mp, step, 0, unroll=4)


def pack(tile_of, own, above, below, devices_mp, capacity):
    tile_rows, sub_rows, width = own.shape
    vmem = pl.BlockSpec(memory_space=pltpu.VMEM)
    return pl.pallas_call(
        pack_kernel,
        in_specs=[pl.BlockSpec(memory_space=pltpu.SMEM), vmem, vmem, vmem],
        out_specs=vmem,
        out_shape=jax.ShapeDtypeStruct((devices_mp, capacity, sub_rows, width // 2), bf16),
        scratch_shapes=[pltpu.VMEM((2 * tile_rows, sub_rows, width // 2), bf16)],
        compiler_params=pltpu.CompilerParams(vmem_limit_bytes=VMEM_LIMIT),
        name="pack",
    )(tile_of, own, above, below)


def dot(a, b):
    return jnp.dot(a, b, preferred_element_type=f32)


def prepare_kernel(
    left_hbm, right_hbm, first_hbm, second_hbm, left, left_t, right, right_t, first, second, sems
):
    pairs = ((left_hbm, left), (right_hbm, right), (first_hbm, first), (second_hbm, second))
    copies = [pltpu.make_async_copy(a, b, sems.at[k]) for k, (a, b) in enumerate(pairs)]
    for copy in copies:
        copy.start()
    capacity = left.shape[0]
    copies[0].wait()
    for s in range(capacity):
        left_t[s] = left[s].T
    copies[1].wait()
    for s in range(capacity):
        right_t[s] = right[s].T
    copies[2].wait()
    copies[3].wait()


def prepare(left, right, first, second):
    hbm = pl.BlockSpec(memory_space=pl.ANY)
    vmem = pl.BlockSpec(memory_space=pltpu.VMEM)
    square, wide = pltpu.VMEM(left.shape, bf16), pltpu.VMEM(left.shape, f32)
    return pl.pallas_call(
        prepare_kernel,
        in_specs=[hbm] * 4,
        out_specs=(vmem,) * 6,
        out_shape=(square, square, square, square, square, wide),
        scratch_shapes=[pltpu.SemaphoreType.DMA((4,))],
        compiler_params=pltpu.CompilerParams(vmem_limit_bytes=SMALL_VMEM),
        name="prepare",
    )(left, right, first, second)


def tile_kernel(
    held_ref, terms_ref, grad, left, left_t, right, right_t, first, second,
    update, first_out_hbm, second_out_hbm, first_out, second_out, sems,
):
    capacity, size, _ = left.shape

    def drain(s):
        return (
            pltpu.make_async_copy(first_out.at[s], first_out_hbm.at[s], sems.at[s, 0]),
            pltpu.make_async_copy(second_out.at[s], second_out_hbm.at[s], sems.at[s, 1]),
        )

    for s in range(capacity):
        occupied = s < held_ref[0]

        @pl.when(occupied)
        def _():
            tile = grad[:, s].reshape(size, size)
            projected = dot(left_t[s], tile).astype(bf16)
            rotated = dot(projected, right[s])
            first_new = beta_first * first[s].astype(f32) + (1.0 - beta_first) * rotated
            second_new = beta_second * second[s] + (1.0 - beta_second) * rotated * rotated
            first_out[s] = first_new.astype(bf16)
            second_out[s] = second_new
            direction = (
                first_new / terms_ref[1] / (jnp.sqrt(second_new / terms_ref[2]) + epsilon)
            ).astype(bf16)
            returned = dot(left[s], direction).astype(bf16)
            step = (terms_ref[0] * dot(returned, right_t[s])).astype(bf16)
            update[:, s] = step.reshape(grad.shape[0], grad.shape[2], size)

        @pl.when(jnp.logical_not(occupied))
        def _():
            first_out[s] = first[s]
            second_out[s] = second[s]
            update[:, s] = jnp.zeros((grad.shape[0], grad.shape[2], size), bf16)

        for copy in drain(s):
            copy.start()
    for s in range(capacity):
        for copy in drain(s):
            copy.wait()


def tile_update(held, terms, grads, ready):
    shape = ready[0].shape
    smem = pl.BlockSpec(memory_space=pltpu.SMEM)
    vmem = pl.BlockSpec(memory_space=pltpu.VMEM)
    hbm = pl.BlockSpec(memory_space=pl.ANY)
    return pl.pallas_call(
        tile_kernel,
        in_specs=[smem, smem] + [vmem] * 7,
        out_specs=(vmem, hbm, hbm),
        out_shape=(
            jax.ShapeDtypeStruct(grads.shape, bf16),
            jax.ShapeDtypeStruct(shape, bf16),
            jax.ShapeDtypeStruct(shape, f32),
        ),
        scratch_shapes=[
            pltpu.VMEM(shape, bf16),
            pltpu.VMEM(shape, f32),
            pltpu.SemaphoreType.DMA((shape[0], 2)),
        ],
        compiler_params=pltpu.CompilerParams(vmem_limit_bytes=TILE_VMEM),
        name="tile_update",
    )(held, terms, grads, *ready)


def place_kernel(slot_of_ref, back_ref, out_ref):
    tile_rows, sub_rows, width = out_ref.shape
    half = width // 2

    def step(l, carry):
        out_ref[l, :, :half] = back_ref[slot_of_ref[2 * l]]
        out_ref[l, :, half:] = back_ref[slot_of_ref[2 * l + 1]]
        return carry

    lax.fori_loop(0, tile_rows, step, 0, unroll=4)


def place(slot_of, back, tile_rows):
    slots, sub_rows, size = back.shape
    vmem = pl.BlockSpec(memory_space=pltpu.VMEM)
    return pl.pallas_call(
        place_kernel,
        in_specs=[pl.BlockSpec(memory_space=pltpu.SMEM), vmem],
        out_specs=vmem,
        out_shape=jax.ShapeDtypeStruct((tile_rows, sub_rows, 2 * size), bf16),
        compiler_params=pltpu.CompilerParams(vmem_limit_bytes=VMEM_LIMIT),
        name="place",
    )(slot_of, back)


def together(*values):
    return lax.optimization_barrier(values)


def body(partials, owners, step_count, basis_left, basis_right, moment_first, moment_second):
    replicas = lax.axis_size("replica")
    devices_mp = lax.axis_size("mp")
    replica_id = lax.axis_index("replica").astype(jnp.int32)
    my_index = lax.axis_index("mp").astype(jnp.int32)
    part = partials[0]
    tile_rows, sub_rows, columns = part.shape
    capacity = basis_left.shape[2]
    width = columns // replicas
    half = width // 2
    far = replicas // 2
    up = [(i, (i + 1) % replicas) for i in range(replicas)]
    down = [(i, (i - 1) % replicas) for i in range(replicas)]

    def block(offset, start, size):
        column = lax.rem(replica_id + offset + replicas, replicas) * width + start
        return lax.dynamic_slice(part, (0, 0, column), (tile_rows, sub_rows, size))

    def swap(low, high):
        return lax.ppermute(low, "replica", down), lax.ppermute(high, "replica", up)

    low, high = together(block(far, 0, half), block(far, half, half))
    above, below = swap(low, high)
    state = (owners, step_count, basis_left[0, 0], basis_right[0, 0], moment_first[0, 0], moment_second[0, 0])
    for hops in range(far - 1, 0, -1):
        low, high = together(block(-hops, 0, width), block(hops, 0, width))
        if hops == far - 1:
            low = jnp.concatenate([low[..., :half] + above, low[..., half:]], axis=2)
            high = jnp.concatenate([high[..., :half], high[..., half:] + below], axis=2)
        else:
            low, high = low + above, high + below
        low, high, state = together(low, high, state)
        above, below = swap(low, high)
        if hops == far - 1:
            owners, step_count, *operands = state
            plan = make_plan(owners, replica_id, my_index, devices_mp, capacity)
            step_value = step_count.astype(f32)
            factor = 1.0 - (step_value - decay_start) / decay_length
            first_fix = 1.0 - jnp.power(f32(beta_first), step_value)
            second_fix = 1.0 - jnp.power(f32(beta_second), step_value)
            terms = jnp.stack([-factor, first_fix, second_fix])
            state = (plan, terms, operands)
        elif hops == far - 2:
            plan, terms, operands = state
            own = block(0, 0, width)
            state = (plan, terms, prepare(*operands), own)
    (tile_of, slot_of, held), terms, ready, own = state
    outgoing = pack(tile_of, own, above, below, devices_mp, capacity)
    arrived = lax.all_to_all(outgoing, "mp", split_axis=0, concat_axis=0, tiled=True)
    update, first_out, second_out = tile_update(held, terms, arrived, ready)
    back = lax.all_to_all(update, "mp", split_axis=0, concat_axis=0, tiled=True)
    slab = place(slot_of, back.reshape(devices_mp * capacity, sub_rows, half), tile_rows)
    return slab, first_out[None, None], second_out[None, None]


def solution(mesh):
    in_specs = (
        P("replica", None, "mp", None),
        P(),
        P(),
        P("replica", "mp", None, None, None),
        P("replica", "mp", None, None, None),
        P("replica", "mp", None, None, None),
        P("replica", "mp", None, None, None),
    )
    out_specs = (
        P(None, "mp", "replica"),
        P("replica", "mp", None, None, None),
        P("replica", "mp", None, None, None),
    )
    return jax.shard_map(body, mesh=mesh, in_specs=in_specs, out_specs=out_specs, check_vma=False)
```

```python
import functools
import jax
import jax.numpy as jnp
from jax import lax
from jax.experimental import pallas as pl
from jax.experimental.pallas import tpu as pltpu
from jax.sharding import PartitionSpec as P

bf16 = jnp.bfloat16
f32 = jnp.float32
beta_first = 0.9
beta_second = 0.95
epsilon = 1e-08
decay_start = 9000.0
decay_length = 1000.0
MIB = 1024 * 1024
VMEM_LIMIT = 16 * MIB
TILE_VMEM = 32 * MIB
SMALL_VMEM = 16 * MIB


def plan_kernel(devices_mp, capacity, owners_ref, tile_of_ref, slot_of_ref, held_ref):
    replica_id, my_index = lax.axis_index("replica"), lax.axis_index("mp")
    tiles = slot_of_ref.shape[0]
    for i in range(devices_mp * capacity):
        tile_of_ref[i] = 0
    counts = tile_of_ref.shape[0] - devices_mp
    for m in range(devices_mp):
        tile_of_ref[counts + m] = 0

    def step(t, carry):
        owner = owners_ref[replica_id * tiles + t]
        rank = tile_of_ref[counts + owner]
        tile_of_ref[counts + owner] = rank + 1
        slot = owner * capacity + rank
        tile_of_ref[slot] = t
        slot_of_ref[t] = slot
        return carry

    lax.fori_loop(0, tiles, step, 0)
    held_ref[0] = tile_of_ref[counts + my_index]


def make_plan(owners, devices_mp, capacity):
    tiles = owners.shape[1] * owners.shape[2]
    smem = pl.BlockSpec(memory_space=pltpu.SMEM)
    return pl.pallas_call(
        functools.partial(plan_kernel, devices_mp, capacity),
        out_shape=(
            jax.ShapeDtypeStruct((devices_mp * (capacity + 1),), jnp.int32),
            jax.ShapeDtypeStruct((tiles,), jnp.int32),
            jax.ShapeDtypeStruct((1,), jnp.int32),
        ),
        in_specs=[smem],
        out_specs=(smem, smem, smem),
        name="plan",
    )(owners.reshape(-1))


def block_kernel(blocks, replicas, width, part_ref, *refs):
    replica_id = lax.axis_index("replica")
    outs, sems = refs[:-1], refs[-1]
    copies = []
    for k, (offset, start, size) in enumerate(blocks):
        column = lax.rem(replica_id + offset + replicas, replicas) * width + start
        source = part_ref.at[:, :, pl.ds(pl.multiple_of(column, 128), size)]
        copies.append(pltpu.make_async_copy(source, outs[k], sems.at[k]))
    for copy in copies:
        copy.start()
    for copy in copies:
        copy.wait()


def fetch_blocks(part, replicas, width, blocks, name):
    shapes = tuple(pltpu.VMEM(part.shape[:2] + (size,), part.dtype) for _, _, size in blocks)
    return pl.pallas_call(
        functools.partial(block_kernel, blocks, replicas, width),
        in_specs=[pl.BlockSpec(memory_space=pl.ANY)],
        out_specs=(pl.BlockSpec(memory_space=pltpu.VMEM),) * len(blocks),
        out_shape=shapes,
        scratch_shapes=[pltpu.SemaphoreType.DMA((len(blocks),))],
        compiler_params=pltpu.CompilerParams(vmem_limit_bytes=SMALL_VMEM),
        name=name,
    )(pltpu.with_memory_space_constraint(part, pltpu.HBM))


def pack_kernel(tile_of_ref, own_ref, above_ref, below_ref, out_ref, sums_ref):
    tile_rows, sub_rows, width = own_ref.shape
    half = width // 2
    for l in range(tile_rows):
        total = (
            own_ref[l].astype(f32) + above_ref[l].astype(f32) + below_ref[l].astype(f32)
        ).astype(bf16)
        sums_ref[2 * l] = total[:, :half]
        sums_ref[2 * l + 1] = total[:, half:]
    devices_mp, capacity = out_ref.shape[:2]

    def step(m, carry):
        for c in range(capacity):
            out_ref[m, c] = sums_ref[tile_of_ref[m * capacity + c]]
        return carry

    lax.fori_loop(0, devices_mp, step, 0, unroll=4)


def pack(tile_of, own, above, below, devices_mp, capacity):
    tile_rows, sub_rows, width = own.shape
    vmem = pl.BlockSpec(memory_space=pltpu.VMEM)
    return pl.pallas_call(
        pack_kernel,
        in_specs=[pl.BlockSpec(memory_space=pltpu.SMEM), vmem, vmem, vmem],
        out_specs=vmem,
        out_shape=jax.ShapeDtypeStruct((devices_mp, capacity, sub_rows, width // 2), bf16),
        scratch_shapes=[pltpu.VMEM((2 * tile_rows, sub_rows, width // 2), bf16)],
        compiler_params=pltpu.CompilerParams(vmem_limit_bytes=VMEM_LIMIT),
        name="pack",
    )(tile_of, own, above, below)


def dot(a, b):
    return jnp.dot(a, b, preferred_element_type=f32)


def prepare_kernel(
    left_hbm, right_hbm, first_hbm, second_hbm, left, left_t, right, right_t, first, second, sems
):
    pairs = ((left_hbm, left), (right_hbm, right), (first_hbm, first), (second_hbm, second))
    copies = [pltpu.make_async_copy(a, b, sems.at[k]) for k, (a, b) in enumerate(pairs)]
    for copy in copies:
        copy.start()
    capacity = left.shape[0]
    copies[0].wait()
    for s in range(capacity):
        left_t[s] = left[s].T
    copies[1].wait()
    for s in range(capacity):
        right_t[s] = right[s].T
    copies[2].wait()
    copies[3].wait()


def prepare(left, right, first, second):
    hbm = pl.BlockSpec(memory_space=pl.ANY)
    vmem = pl.BlockSpec(memory_space=pltpu.VMEM)
    square, wide = pltpu.VMEM(left.shape, bf16), pltpu.VMEM(left.shape, f32)
    return pl.pallas_call(
        prepare_kernel,
        in_specs=[hbm] * 4,
        out_specs=(vmem,) * 6,
        out_shape=(square, square, square, square, square, wide),
        scratch_shapes=[pltpu.SemaphoreType.DMA((4,))],
        compiler_params=pltpu.CompilerParams(vmem_limit_bytes=SMALL_VMEM),
        name="prepare",
    )(*(pltpu.with_memory_space_constraint(a, pltpu.HBM) for a in (left, right, first, second)))


def tile_kernel(
    held_ref, terms_ref, grad, left, left_t, right, right_t, first, second,
    update, first_out_hbm, second_out_hbm, first_out, second_out, sems,
):
    capacity, size, _ = left.shape

    def drain(s):
        return (
            pltpu.make_async_copy(first_out.at[s], first_out_hbm.at[s], sems.at[s, 0]),
            pltpu.make_async_copy(second_out.at[s], second_out_hbm.at[s], sems.at[s, 1]),
        )

    for s in range(capacity):
        occupied = s < held_ref[0]

        @pl.when(occupied)
        def _():
            tile = grad[:, s].reshape(size, size)
            projected = dot(left_t[s], tile).astype(bf16)
            rotated = dot(projected, right[s])
            first_new = beta_first * first[s].astype(f32) + (1.0 - beta_first) * rotated
            second_new = beta_second * second[s] + (1.0 - beta_second) * rotated * rotated
            first_out[s] = first_new.astype(bf16)
            second_out[s] = second_new
            direction = (
                first_new / terms_ref[1] / (jnp.sqrt(second_new / terms_ref[2]) + epsilon)
            ).astype(bf16)
            returned = dot(left[s], direction).astype(bf16)
            step = (terms_ref[0] * dot(returned, right_t[s])).astype(bf16)
            update[:, s] = step.reshape(grad.shape[0], grad.shape[2], size)

        @pl.when(jnp.logical_not(occupied))
        def _():
            first_out[s] = first[s]
            second_out[s] = second[s]
            update[:, s] = jnp.zeros((grad.shape[0], grad.shape[2], size), bf16)

        for copy in drain(s):
            copy.start()
    for s in range(capacity):
        for copy in drain(s):
            copy.wait()


def tile_update(held, terms, grads, ready):
    shape = ready[0].shape
    smem = pl.BlockSpec(memory_space=pltpu.SMEM)
    vmem = pl.BlockSpec(memory_space=pltpu.VMEM)
    hbm = pl.BlockSpec(memory_space=pl.ANY)
    return pl.pallas_call(
        tile_kernel,
        in_specs=[smem, smem] + [vmem] * 7,
        out_specs=(vmem, hbm, hbm),
        out_shape=(
            jax.ShapeDtypeStruct(grads.shape, bf16),
            jax.ShapeDtypeStruct(shape, bf16),
            jax.ShapeDtypeStruct(shape, f32),
        ),
        scratch_shapes=[
            pltpu.VMEM(shape, bf16),
            pltpu.VMEM(shape, f32),
            pltpu.SemaphoreType.DMA((shape[0], 2)),
        ],
        compiler_params=pltpu.CompilerParams(vmem_limit_bytes=TILE_VMEM),
        name="tile_update",
    )(held, terms, grads, *ready)


def place_kernel(slot_of_ref, back_ref, out_ref):
    tile_rows, sub_rows, width = out_ref.shape
    half = width // 2

    def step(l, carry):
        out_ref[l, :, :half] = back_ref[slot_of_ref[2 * l]]
        out_ref[l, :, half:] = back_ref[slot_of_ref[2 * l + 1]]
        return carry

    lax.fori_loop(0, tile_rows, step, 0, unroll=4)


def place(slot_of, back, tile_rows):
    slots, sub_rows, size = back.shape
    vmem = pl.BlockSpec(memory_space=pltpu.VMEM)
    return pl.pallas_call(
        place_kernel,
        in_specs=[pl.BlockSpec(memory_space=pltpu.SMEM), vmem],
        out_specs=vmem,
        out_shape=jax.ShapeDtypeStruct((tile_rows, sub_rows, 2 * size), bf16),
        compiler_params=pltpu.CompilerParams(vmem_limit_bytes=VMEM_LIMIT),
        name="place",
    )(slot_of, back)


def together(*values):
    return lax.optimization_barrier(values)


def body(partials, owners, step_count, basis_left, basis_right, moment_first, moment_second):
    replicas = lax.axis_size("replica")
    devices_mp = lax.axis_size("mp")
    part = partials[0]
    tile_rows, sub_rows, columns = part.shape
    capacity = basis_left.shape[2]
    width = columns // replicas
    half = width // 2
    far = replicas // 2
    up = [(i, (i + 1) % replicas) for i in range(replicas)]
    down = [(i, (i - 1) % replicas) for i in range(replicas)]

    def swap(low, high):
        return lax.ppermute(low, "replica", down), lax.ppermute(high, "replica", up)

    low, high = fetch_blocks(part, replicas, width, ((far, 0, half), (far, half, half)), "first_blocks")
    above, below = swap(low, high)
    low, part = together(low, part)
    order = [(sign * hops, 0, width) for hops in range(far - 1, 0, -1) for sign in (-1, 1)]
    *blocks, own = fetch_blocks(part, replicas, width, (*order, (0, 0, width)), "rest_blocks")
    state = (owners, step_count, basis_left[0, 0], basis_right[0, 0], moment_first[0, 0], moment_second[0, 0])
    for hops in range(far - 1, 0, -1):
        low, high, *blocks = blocks
        if hops == far - 1:
            low = jnp.concatenate([low[..., :half] + above, low[..., half:]], axis=2)
            high = jnp.concatenate([high[..., :half], high[..., half:] + below], axis=2)
        else:
            low, high = low + above, high + below
        low, high, state = together(low, high, state)
        above, below = swap(low, high)
        if hops == far - 1:
            owners, step_count, *operands = state
            plan = make_plan(owners, devices_mp, capacity)
            step_value = step_count.astype(f32)
            factor = 1.0 - (step_value - decay_start) / decay_length
            first_fix = 1.0 - jnp.power(f32(beta_first), step_value)
            second_fix = 1.0 - jnp.power(f32(beta_second), step_value)
            terms = jnp.stack([-factor, first_fix, second_fix])
            state = (plan, terms, operands)
        elif hops == far - 2:
            plan, terms, operands = state
            state = (plan, terms, prepare(*operands))
    (tile_of, slot_of, held), terms, ready = state
    outgoing = pack(tile_of, own, above, below, devices_mp, capacity)
    arrived = lax.all_to_all(outgoing, "mp", split_axis=0, concat_axis=0, tiled=True)
    update, first_out, second_out = tile_update(held, terms, arrived, ready)
    back = lax.all_to_all(update, "mp", split_axis=0, concat_axis=0, tiled=True)
    slab = place(slot_of, back.reshape(devices_mp * capacity, sub_rows, half), tile_rows)
    return slab, first_out[None, None], second_out[None, None]


def solution(mesh):
    in_specs = (
        P("replica", None, "mp", None),
        P(),
        P(),
        P("replica", "mp", None, None, None),
        P("replica", "mp", None, None, None),
        P("replica", "mp", None, None, None),
        P("replica", "mp", None, None, None),
    )
    out_specs = (
        P(None, "mp", "replica"),
        P("replica", "mp", None, None, None),
        P("replica", "mp", None, None, None),
    )
    return jax.shard_map(body, mesh=mesh, in_specs=in_specs, out_specs=out_specs, check_vma=False)
```

```python
import functools
import jax
import jax.numpy as jnp
from jax import lax
from jax.experimental import pallas as pl
from jax.experimental.pallas import tpu as pltpu
from jax.sharding import PartitionSpec as P

bf16 = jnp.bfloat16
f32 = jnp.float32
beta_first = 0.9
beta_second = 0.95
epsilon = 1e-08
decay_start = 9000.0
decay_length = 1000.0
MIB = 1024 * 1024
VMEM_LIMIT = 16 * MIB
TILE_VMEM = 32 * MIB
SMALL_VMEM = 16 * MIB


def plan_kernel(devices_mp, capacity, owners_ref, tile_of_ref, slot_of_ref, held_ref):
    replica_id, my_index = lax.axis_index("replica"), lax.axis_index("mp")
    tiles = slot_of_ref.shape[0]
    for i in range(devices_mp * capacity):
        tile_of_ref[i] = 0
    counts = tile_of_ref.shape[0] - devices_mp
    for m in range(devices_mp):
        tile_of_ref[counts + m] = 0

    def step(t, carry):
        owner = owners_ref[replica_id * tiles + t]
        rank = tile_of_ref[counts + owner]
        tile_of_ref[counts + owner] = rank + 1
        slot = owner * capacity + rank
        tile_of_ref[slot] = t
        slot_of_ref[t] = slot
        return carry

    lax.fori_loop(0, tiles, step, 0)
    held_ref[0] = tile_of_ref[counts + my_index]


def make_plan(owners, devices_mp, capacity):
    tiles = owners.shape[1] * owners.shape[2]
    smem = pl.BlockSpec(memory_space=pltpu.SMEM)
    return pl.pallas_call(
        functools.partial(plan_kernel, devices_mp, capacity),
        out_shape=(
            jax.ShapeDtypeStruct((devices_mp * (capacity + 1),), jnp.int32),
            jax.ShapeDtypeStruct((tiles,), jnp.int32),
            jax.ShapeDtypeStruct((1,), jnp.int32),
        ),
        in_specs=[smem],
        out_specs=(smem, smem, smem),
        name="plan",
    )(owners.reshape(-1))


def block_kernel(blocks, replicas, width, part_ref, *refs):
    replica_id = lax.axis_index("replica")
    outs, sems = refs[:-1], refs[-1]
    copies = []
    for k, (offset, start, size) in enumerate(blocks):
        column = lax.rem(replica_id + offset + replicas, replicas) * width + start
        source = part_ref.at[:, :, pl.ds(pl.multiple_of(column, 128), size)]
        copies.append(pltpu.make_async_copy(source, outs[k], sems.at[k]))
    for copy in copies:
        copy.start()
    for copy in copies:
        copy.wait()


def fetch_blocks(part, replicas, width, blocks, name):
    shapes = tuple(pltpu.VMEM(part.shape[:2] + (size,), part.dtype) for _, _, size in blocks)
    return pl.pallas_call(
        functools.partial(block_kernel, blocks, replicas, width),
        in_specs=[pl.BlockSpec(memory_space=pl.ANY)],
        out_specs=(pl.BlockSpec(memory_space=pltpu.VMEM),) * len(blocks),
        out_shape=shapes,
        scratch_shapes=[pltpu.SemaphoreType.DMA((len(blocks),))],
        compiler_params=pltpu.CompilerParams(vmem_limit_bytes=SMALL_VMEM),
        name=name,
    )(pltpu.with_memory_space_constraint(part, pltpu.HBM))


def add_kernel(start, block_ref, arrived_ref, out_ref):
    rows, _, width = block_ref.shape
    size = arrived_ref.shape[2]
    cols = slice(start, start + size)
    rest = slice(0, start) if start else slice(size, width)
    for l in range(rows):
        out_ref[l, :, cols] = block_ref[l, :, cols] + arrived_ref[l]
        if size < width:
            out_ref[l, :, rest] = block_ref[l, :, rest]


def add_block(block, arrived, start):
    vmem = pl.BlockSpec(memory_space=pltpu.VMEM)
    return pl.pallas_call(
        functools.partial(add_kernel, start),
        in_specs=[vmem, vmem],
        out_specs=vmem,
        out_shape=pltpu.VMEM(block.shape, block.dtype),
        compiler_params=pltpu.CompilerParams(vmem_limit_bytes=SMALL_VMEM),
        name="add_block",
    )(block, pltpu.with_memory_space_constraint(arrived, pltpu.VMEM))


def pack_kernel(tile_of_ref, own_ref, above_ref, below_ref, out_ref, sums_ref):
    tile_rows, sub_rows, width = own_ref.shape
    half = width // 2
    for l in range(tile_rows):
        total = (
            own_ref[l].astype(f32) + above_ref[l].astype(f32) + below_ref[l].astype(f32)
        ).astype(bf16)
        sums_ref[2 * l] = total[:, :half]
        sums_ref[2 * l + 1] = total[:, half:]
    devices_mp, capacity = out_ref.shape[:2]

    def step(m, carry):
        for c in range(capacity):
            out_ref[m, c] = sums_ref[tile_of_ref[m * capacity + c]]
        return carry

    lax.fori_loop(0, devices_mp, step, 0, unroll=4)


def pack(tile_of, own, above, below, devices_mp, capacity):
    tile_rows, sub_rows, width = own.shape
    vmem = pl.BlockSpec(memory_space=pltpu.VMEM)
    return pl.pallas_call(
        pack_kernel,
        in_specs=[pl.BlockSpec(memory_space=pltpu.SMEM), vmem, vmem, vmem],
        out_specs=vmem,
        out_shape=jax.ShapeDtypeStruct((devices_mp, capacity, sub_rows, width // 2), bf16),
        scratch_shapes=[pltpu.VMEM((2 * tile_rows, sub_rows, width // 2), bf16)],
        compiler_params=pltpu.CompilerParams(vmem_limit_bytes=VMEM_LIMIT),
        name="pack",
    )(tile_of, own, above, below)


def dot(a, b):
    return jnp.dot(a, b, preferred_element_type=f32)


def prepare_kernel(
    left_hbm, right_hbm, first_hbm, second_hbm, left, left_t, right, right_t, first, second, sems
):
    pairs = ((left_hbm, left), (right_hbm, right), (first_hbm, first), (second_hbm, second))
    copies = [pltpu.make_async_copy(a, b, sems.at[k]) for k, (a, b) in enumerate(pairs)]
    for copy in copies:
        copy.start()
    capacity = left.shape[0]
    copies[0].wait()
    for s in range(capacity):
        left_t[s] = left[s].T
    copies[1].wait()
    for s in range(capacity):
        right_t[s] = right[s].T
    copies[2].wait()
    copies[3].wait()


def prepare(left, right, first, second):
    hbm = pl.BlockSpec(memory_space=pl.ANY)
    vmem = pl.BlockSpec(memory_space=pltpu.VMEM)
    square, wide = pltpu.VMEM(left.shape, bf16), pltpu.VMEM(left.shape, f32)
    return pl.pallas_call(
        prepare_kernel,
        in_specs=[hbm] * 4,
        out_specs=(vmem,) * 6,
        out_shape=(square, square, square, square, square, wide),
        scratch_shapes=[pltpu.SemaphoreType.DMA((4,))],
        compiler_params=pltpu.CompilerParams(vmem_limit_bytes=SMALL_VMEM),
        name="prepare",
    )(*(pltpu.with_memory_space_constraint(a, pltpu.HBM) for a in (left, right, first, second)))


def tile_kernel(
    held_ref, terms_ref, grad, left, left_t, right, right_t, first, second,
    update, first_out, second_out, returned,
):
    capacity, size, _ = left.shape
    devices_mp, _, sub_rows, _ = grad.shape
    half = size // 2
    scale, first_fix, second_fix = terms_ref[0], terms_ref[1], terms_ref[2]

    def work(slots):
        projected = {
            s: dot(left_t[s], grad[:, s].reshape(size, size)).astype(bf16) for s in slots
        }
        for start in (0, half):
            cols = slice(start, start + half)
            for s in slots:
                rotated = dot(projected[s], right[s, :, cols])
                first_new = (
                    beta_first * first[s, :, cols].astype(f32) + (1.0 - beta_first) * rotated
                )
                second_new = (
                    beta_second * second[s, :, cols] + (1.0 - beta_second) * rotated * rotated
                )
                first_out[s, :, cols] = first_new.astype(bf16)
                second_out[s, :, cols] = second_new
                direction = (
                    first_new * first_fix / (jnp.sqrt(second_new * second_fix) + epsilon)
                ).astype(bf16)
                returned[s, :, cols] = dot(left[s], direction).astype(bf16)
        for s in slots:
            step = (scale * dot(returned[s], right_t[s])).astype(bf16)
            update[:, s] = step.reshape(devices_mp, sub_rows, size)

    def keep(slots):
        for s in slots:
            first_out[s] = first[s]
            second_out[s] = second[s]
            update[:, s] = jnp.zeros((devices_mp, sub_rows, size), bf16)

    for count in range(capacity + 1):

        @pl.when(held_ref[0] == count)
        def _():
            work(range(count))
            keep(range(count, capacity))


def tile_update(held, terms, grads, ready):
    shape = ready[0].shape
    smem = pl.BlockSpec(memory_space=pltpu.SMEM)
    vmem = pl.BlockSpec(memory_space=pltpu.VMEM)
    return pl.pallas_call(
        tile_kernel,
        in_specs=[smem, smem] + [vmem] * 7,
        out_specs=(vmem, vmem, vmem),
        out_shape=(pltpu.VMEM(grads.shape, bf16), pltpu.VMEM(shape, bf16), pltpu.VMEM(shape, f32)),
        scratch_shapes=[pltpu.VMEM(shape, bf16)],
        compiler_params=pltpu.CompilerParams(vmem_limit_bytes=TILE_VMEM),
        name="tile_update",
    )(held, terms, grads, *ready)


def place_kernel(
    slot_of_ref, back_ref, first_ref, second_ref, out_ref, first_hbm, second_hbm, sems
):
    tile_rows, sub_rows, width = out_ref.shape
    half = width // 2
    copies = (
        pltpu.make_async_copy(second_ref, second_hbm, sems.at[0]),
        pltpu.make_async_copy(first_ref, first_hbm, sems.at[1]),
    )
    for copy in copies:
        copy.start()

    def step(l, carry):
        out_ref[l, :, :half] = back_ref[slot_of_ref[2 * l]]
        out_ref[l, :, half:] = back_ref[slot_of_ref[2 * l + 1]]
        return carry

    lax.fori_loop(0, tile_rows, step, 0, unroll=4)
    for copy in copies:
        copy.wait()


def place(slot_of, back, first, second, tile_rows):
    slots, sub_rows, size = back.shape
    vmem = pl.BlockSpec(memory_space=pltpu.VMEM)
    hbm = pl.BlockSpec(memory_space=pl.ANY)
    return pl.pallas_call(
        place_kernel,
        in_specs=[pl.BlockSpec(memory_space=pltpu.SMEM), vmem, vmem, vmem],
        out_specs=(vmem, hbm, hbm),
        out_shape=(
            jax.ShapeDtypeStruct((tile_rows, sub_rows, 2 * size), bf16),
            jax.ShapeDtypeStruct(first.shape, bf16),
            jax.ShapeDtypeStruct(second.shape, f32),
        ),
        scratch_shapes=[pltpu.SemaphoreType.DMA((2,))],
        compiler_params=pltpu.CompilerParams(vmem_limit_bytes=VMEM_LIMIT),
        name="place",
    )(slot_of, back, first, second)


def together(*values):
    return lax.optimization_barrier(values)


def body(partials, owners, step_count, basis_left, basis_right, moment_first, moment_second):
    replicas = lax.axis_size("replica")
    devices_mp = lax.axis_size("mp")
    part = partials[0]
    tile_rows, sub_rows, columns = part.shape
    capacity = basis_left.shape[2]
    width = columns // replicas
    half = width // 2
    far = replicas // 2
    up = [(i, (i + 1) % replicas) for i in range(replicas)]
    down = [(i, (i - 1) % replicas) for i in range(replicas)]

    def swap(low, high):
        return lax.ppermute(low, "replica", down), lax.ppermute(high, "replica", up)

    low, high = fetch_blocks(part, replicas, width, ((far, 0, half), (far, half, half)), "first_blocks")
    above, below = swap(low, high)
    low, part = together(low, part)
    order = [(sign * hops, 0, width) for hops in range(far - 1, 0, -1) for sign in (-1, 1)]
    *blocks, own = fetch_blocks(part, replicas, width, (*order, (0, 0, width)), "rest_blocks")
    state = (owners, step_count, basis_left[0, 0], basis_right[0, 0], moment_first[0, 0], moment_second[0, 0])
    for hops in range(far - 1, 0, -1):
        low, high, *blocks = blocks
        low = add_block(low, above, 0)
        high = add_block(high, below, half if hops == far - 1 else 0)
        low, state = together(low, state)
        above, below = swap(low, high)
        if hops == far - 1:
            owners, step_count, *operands = state
            plan = make_plan(owners, devices_mp, capacity)
            step_value = step_count.astype(f32)
            factor = 1.0 - (step_value - decay_start) / decay_length
            first_fix = 1.0 - jnp.power(f32(beta_first), step_value)
            second_fix = 1.0 - jnp.power(f32(beta_second), step_value)
            terms = jnp.stack([-factor, 1.0 / first_fix, 1.0 / second_fix])
            state = (plan, terms, operands)
        elif hops == far - 2:
            plan, terms, operands = state
            state = (plan, terms, prepare(*operands))
    (tile_of, slot_of, held), terms, ready = state
    outgoing = pack(tile_of, own, above, below, devices_mp, capacity)
    arrived = lax.all_to_all(outgoing, "mp", split_axis=0, concat_axis=0, tiled=True)
    update, first_out, second_out = tile_update(held, terms, arrived, ready)
    back = lax.all_to_all(update, "mp", split_axis=0, concat_axis=0, tiled=True)
    back = back.reshape(devices_mp * capacity, sub_rows, half)
    slab, first_out, second_out = place(slot_of, back, first_out, second_out, tile_rows)
    return slab, first_out[None, None], second_out[None, None]


def solution(mesh):
    in_specs = (
        P("replica", None, "mp", None),
        P(),
        P(),
        P("replica", "mp", None, None, None),
        P("replica", "mp", None, None, None),
        P("replica", "mp", None, None, None),
        P("replica", "mp", None, None, None),
    )
    out_specs = (
        P(None, "mp", "replica"),
        P("replica", "mp", None, None, None),
        P("replica", "mp", None, None, None),
    )
    return jax.shard_map(body, mesh=mesh, in_specs=in_specs, out_specs=out_specs, check_vma=False)
```

```python
import functools
import math
import jax
import jax.numpy as jnp
from jax import lax
from jax.experimental import pallas as pl
from jax.experimental.pallas import tpu as pltpu
from jax.sharding import PartitionSpec as P

bf16 = jnp.bfloat16
f32 = jnp.float32
beta_first = 0.9
beta_second = 0.95
epsilon = 1e-08
decay_start = 9000.0
decay_length = 1000.0
MIB = 1024 * 1024
VMEM_LIMIT = 12 * MIB
TILE_VMEM = 24 * MIB
SMALL_VMEM = 4 * MIB
PIECES = 4


def plan_kernel(owners_ref, tile_of_ref, slot_of_ref, held_ref):
    replica_id, my_index = lax.axis_index("replica"), lax.axis_index("mp")
    _, tile_cols, tile_rows = owners_ref.shape
    devices_mp = lax.axis_size("mp")
    counts = tile_of_ref.shape[0] - devices_mp
    capacity = counts // devices_mp
    for i in range(tile_of_ref.shape[0]):
        tile_of_ref[i] = 0

    def step(l, carry):
        for j in range(tile_cols):
            owner = owners_ref[replica_id, j, l]
            rank = tile_of_ref[counts + owner]
            tile_of_ref[counts + owner] = rank + 1
            slot = owner * capacity + rank
            tile_of_ref[slot] = l * tile_cols + j
            slot_of_ref[l * tile_cols + j] = slot
        return carry

    lax.fori_loop(0, tile_rows, step, 0)
    held_ref[0] = tile_of_ref[counts + my_index]


def make_plan(owners, devices_mp, capacity):
    tiles = owners.shape[1] * owners.shape[2]
    smem = pl.BlockSpec(memory_space=pltpu.SMEM)
    return pl.pallas_call(
        plan_kernel,
        out_shape=(
            jax.ShapeDtypeStruct((devices_mp * (capacity + 1),), jnp.int32),
            jax.ShapeDtypeStruct((tiles,), jnp.int32),
            jax.ShapeDtypeStruct((1,), jnp.int32),
        ),
        in_specs=[smem],
        out_specs=(smem, smem, smem),
        compiler_params=pltpu.CompilerParams(vmem_limit_bytes=MIB),
        name="plan",
    )(jnp.swapaxes(owners, 1, 2))


def block_kernel(blocks, replicas, width, part_ref, step_ref, *refs):
    replica_id = lax.axis_index("replica")
    *outs, step_out_ref, sems = refs
    step_out_ref[0] = step_ref[0]
    rows = part_ref.shape[0] // PIECES
    copies = []
    for k, (offset, start, size) in enumerate(blocks):
        column = lax.rem(replica_id + offset + replicas, replicas) * width + start
        for p in range(PIECES):
            some = slice(p * rows, (p + 1) * rows)
            source = part_ref.at[some, :, pl.ds(pl.multiple_of(column, 128), size)]
            copies.append(pltpu.make_async_copy(source, outs[k].at[some], sems.at[k, p]))
    for copy in copies:
        copy.start()
    for copy in copies:
        copy.wait()


def fetch_blocks(part, step_count, replicas, width, blocks, name):
    smem = pl.BlockSpec(memory_space=pltpu.SMEM)
    shapes = tuple(pltpu.VMEM(part.shape[:2] + (size,), part.dtype) for _, _, size in blocks)
    return pl.pallas_call(
        functools.partial(block_kernel, blocks, replicas, width),
        in_specs=[pl.BlockSpec(memory_space=pl.ANY), smem],
        out_specs=(pl.BlockSpec(memory_space=pltpu.VMEM),) * len(blocks) + (smem,),
        out_shape=shapes + (jax.ShapeDtypeStruct((1,), jnp.int32),),
        scratch_shapes=[pltpu.SemaphoreType.DMA((len(blocks), PIECES))],
        compiler_params=pltpu.CompilerParams(vmem_limit_bytes=SMALL_VMEM),
        name=name,
    )(pltpu.with_memory_space_constraint(part, pltpu.HBM), step_count)


def add_kernel(start, block_ref, arrived_ref, out_ref):
    rows, _, width = block_ref.shape
    size = arrived_ref.shape[2]
    cols = slice(start, start + size)
    rest = slice(0, start) if start else slice(size, width)
    for l in range(rows):
        out_ref[l, :, cols] = block_ref[l, :, cols] + arrived_ref[l]
        if size < width:
            out_ref[l, :, rest] = block_ref[l, :, rest]


def add_block(block, arrived, start):
    vmem = pl.BlockSpec(memory_space=pltpu.VMEM)
    return pl.pallas_call(
        functools.partial(add_kernel, start),
        in_specs=[vmem, vmem],
        out_specs=vmem,
        out_shape=pltpu.VMEM(block.shape, block.dtype),
        compiler_params=pltpu.CompilerParams(vmem_limit_bytes=SMALL_VMEM),
        name="add_block",
    )(block, pltpu.with_memory_space_constraint(arrived, pltpu.VMEM))


def pack_kernel(tile_of_ref, own_ref, above_ref, below_ref, out_ref, sums_ref):
    tile_rows, sub_rows, width = own_ref.shape
    half = width // 2
    for l in range(tile_rows):
        total = (
            own_ref[l].astype(f32) + above_ref[l].astype(f32) + below_ref[l].astype(f32)
        ).astype(bf16)
        sums_ref[2 * l] = total[:, :half]
        sums_ref[2 * l + 1] = total[:, half:]
    devices_mp, capacity = out_ref.shape[:2]

    def step(m, carry):
        for c in range(capacity):
            out_ref[m, c] = sums_ref[tile_of_ref[m * capacity + c]]
        return carry

    lax.fori_loop(0, devices_mp, step, 0, unroll=4)


def pack(tile_of, own, above, below, devices_mp, capacity):
    tile_rows, sub_rows, width = own.shape
    vmem = pl.BlockSpec(memory_space=pltpu.VMEM)
    return pl.pallas_call(
        pack_kernel,
        in_specs=[pl.BlockSpec(memory_space=pltpu.SMEM), vmem, vmem, vmem],
        out_specs=vmem,
        out_shape=jax.ShapeDtypeStruct((devices_mp, capacity, sub_rows, width // 2), bf16),
        scratch_shapes=[pltpu.VMEM((2 * tile_rows, sub_rows, width // 2), bf16)],
        compiler_params=pltpu.CompilerParams(vmem_limit_bytes=VMEM_LIMIT),
        name="pack",
    )(tile_of, own, above, below)


def dot(a, b):
    return jnp.dot(a, b, preferred_element_type=f32)


def in_pieces(source, target, sems):
    slots, rows, _ = source.shape
    size = rows // PIECES
    return [
        pltpu.make_async_copy(
            source.at[s, pl.ds(p * size, size)], target.at[s, pl.ds(p * size, size)], sems.at[s, p]
        )
        for s in range(slots)
        for p in range(PIECES)
    ]


def prepare_kernel(
    left_hbm, right_hbm, first_hbm, second_hbm, left, left_t, right, right_t, first, second, sems
):
    pairs = ((left_hbm, left), (right_hbm, right), (first_hbm, first), (second_hbm, second))
    arrivals = [in_pieces(a, b, sems.at[k]) for k, (a, b) in enumerate(pairs)]
    for copies in arrivals:
        for copy in copies:
            copy.start()
    for k, copies in enumerate(arrivals):
        for copy in copies:
            copy.wait()
        if k < 2:
            source, target = ((left, left_t), (right, right_t))[k]
            for s in range(source.shape[0]):
                target[s] = source[s].T


def prepare(left, right, first, second):
    hbm = pl.BlockSpec(memory_space=pl.ANY)
    vmem = pl.BlockSpec(memory_space=pltpu.VMEM)
    square, wide = pltpu.VMEM(left.shape, bf16), pltpu.VMEM(left.shape, f32)
    return pl.pallas_call(
        prepare_kernel,
        in_specs=[hbm] * 4,
        out_specs=(vmem,) * 6,
        out_shape=(square, square, square, square, square, wide),
        scratch_shapes=[pltpu.SemaphoreType.DMA((4, left.shape[0], PIECES))],
        compiler_params=pltpu.CompilerParams(vmem_limit_bytes=SMALL_VMEM),
        name="prepare",
    )(*(pltpu.with_memory_space_constraint(a, pltpu.HBM) for a in (left, right, first, second)))


def tile_kernel(
    held_ref, step_ref, grad, left, left_t, right, right_t, first, second,
    update, first_out, second_out, returned,
):
    capacity, size, _ = left.shape
    devices_mp, _, sub_rows, _ = grad.shape
    half = size // 2
    step_value = jnp.full((8, 128), step_ref[0], jnp.int32).astype(f32)
    scale = -(1.0 - (step_value - decay_start) / decay_length)[:1, :1]
    first_fix = (1.0 / (1.0 - jnp.exp(step_value * math.log(beta_first))))[:1, :1]
    second_fix = (1.0 / (1.0 - jnp.exp(step_value * math.log(beta_second))))[:1, :1]

    def work(slots):
        projected = {
            s: dot(left_t[s], grad[:, s].reshape(size, size)).astype(bf16) for s in slots
        }
        for start in (0, half):
            cols = slice(start, start + half)
            for s in slots:
                rotated = dot(projected[s], right[s, :, cols])
                first_new = (
                    beta_first * first[s, :, cols].astype(f32) + (1.0 - beta_first) * rotated
                )
                second_new = (
                    beta_second * second[s, :, cols] + (1.0 - beta_second) * rotated * rotated
                )
                first_out[s, :, cols] = first_new.astype(bf16)
                second_out[s, :, cols] = second_new
                direction = (
                    first_new * first_fix / (jnp.sqrt(second_new * second_fix) + epsilon)
                ).astype(bf16)
                returned[s, :, cols] = dot(left[s], direction).astype(bf16)
        for s in slots:
            step = (scale * dot(returned[s], right_t[s])).astype(bf16)
            update[:, s] = step.reshape(devices_mp, sub_rows, size)

    def keep(slots):
        for s in slots:
            first_out[s] = first[s]
            second_out[s] = second[s]
            update[:, s] = jnp.zeros((devices_mp, sub_rows, size), bf16)

    for count in range(capacity + 1):

        @pl.when(held_ref[0] == count)
        def _():
            work(range(count))
            keep(range(count, capacity))


def tile_update(held, step_count, grads, ready):
    shape = ready[0].shape
    smem = pl.BlockSpec(memory_space=pltpu.SMEM)
    vmem = pl.BlockSpec(memory_space=pltpu.VMEM)
    return pl.pallas_call(
        tile_kernel,
        in_specs=[smem, smem] + [vmem] * 7,
        out_specs=(vmem, vmem, vmem),
        out_shape=(pltpu.VMEM(grads.shape, bf16), pltpu.VMEM(shape, bf16), pltpu.VMEM(shape, f32)),
        scratch_shapes=[pltpu.VMEM(shape, bf16)],
        compiler_params=pltpu.CompilerParams(vmem_limit_bytes=TILE_VMEM),
        name="tile_update",
    )(held, step_count, grads, *ready)


def place_kernel(
    slot_of_ref, back_ref, first_ref, second_ref, out_ref, first_hbm, second_hbm, sems
):
    tile_rows, sub_rows, width = out_ref.shape
    half = width // 2
    copies = in_pieces(second_ref, second_hbm, sems.at[0])
    copies += in_pieces(first_ref, first_hbm, sems.at[1])
    for copy in copies:
        copy.start()

    def step(l, carry):
        out_ref[l, :, :half] = back_ref[slot_of_ref[2 * l]]
        out_ref[l, :, half:] = back_ref[slot_of_ref[2 * l + 1]]
        return carry

    lax.fori_loop(0, tile_rows, step, 0, unroll=4)
    for copy in copies:
        copy.wait()


def place(slot_of, back, first, second, tile_rows):
    slots, sub_rows, size = back.shape
    vmem = pl.BlockSpec(memory_space=pltpu.VMEM)
    hbm = pl.BlockSpec(memory_space=pl.ANY)
    return pl.pallas_call(
        place_kernel,
        in_specs=[pl.BlockSpec(memory_space=pltpu.SMEM), vmem, vmem, vmem],
        out_specs=(vmem, hbm, hbm),
        out_shape=(
            jax.ShapeDtypeStruct((tile_rows, sub_rows, 2 * size), bf16),
            jax.ShapeDtypeStruct(first.shape, bf16),
            jax.ShapeDtypeStruct(second.shape, f32),
        ),
        scratch_shapes=[pltpu.SemaphoreType.DMA((2, first.shape[0], PIECES))],
        compiler_params=pltpu.CompilerParams(vmem_limit_bytes=VMEM_LIMIT),
        name="place",
    )(slot_of, back, first, second)


def together(*values):
    return lax.optimization_barrier(values)


def body(partials, owners, step_count, basis_left, basis_right, moment_first, moment_second):
    replicas = lax.axis_size("replica")
    devices_mp = lax.axis_size("mp")
    part, step_count = partials[0], step_count.reshape(1)
    tile_rows, sub_rows, columns = part.shape
    capacity = basis_left.shape[2]
    width = columns // replicas
    half = width // 2
    far = replicas // 2
    up = [(i, (i + 1) % replicas) for i in range(replicas)]
    down = [(i, (i - 1) % replicas) for i in range(replicas)]

    def swap(low, high):
        return lax.ppermute(low, "replica", down), lax.ppermute(high, "replica", up)

    first = ((far, 0, half), (far, half, half))
    low, high, step_count = fetch_blocks(part, step_count, replicas, width, first, "first_blocks")
    above, below = swap(low, high)
    low, part = together(low, part)
    order = [(sign * hops, 0, width) for hops in range(far - 1, 0, -1) for sign in (-1, 1)]
    rest = (*order, (0, 0, width))
    *blocks, own, step_count = fetch_blocks(part, step_count, replicas, width, rest, "rest_blocks")
    state = (owners, basis_left[0, 0], basis_right[0, 0], moment_first[0, 0], moment_second[0, 0])
    for hops in range(far - 1, 0, -1):
        low, high, *blocks = blocks
        low = add_block(low, above, 0)
        high = add_block(high, below, half if hops == far - 1 else 0)
        low, state = together(low, state)
        above, below = swap(low, high)
        if hops == far - 1:
            owners, *operands = state
            state = (make_plan(owners, devices_mp, capacity), operands)
        elif hops == far - 2:
            plan, operands = state
            state = (plan, prepare(*operands))
    (tile_of, slot_of, held), ready = state
    outgoing = pack(tile_of, own, above, below, devices_mp, capacity)
    arrived = lax.all_to_all(outgoing, "mp", split_axis=0, concat_axis=0, tiled=True)
    update, first_out, second_out = tile_update(held, step_count, arrived, ready)
    back = lax.all_to_all(update, "mp", split_axis=0, concat_axis=0, tiled=True)
    back = back.reshape(devices_mp * capacity, sub_rows, half)
    slab, first_out, second_out = place(slot_of, back, first_out, second_out, tile_rows)
    return slab, first_out[None, None], second_out[None, None]


def solution(mesh):
    in_specs = (
        P("replica", None, "mp", None),
        P(),
        P(),
        P("replica", "mp", None, None, None),
        P("replica", "mp", None, None, None),
        P("replica", "mp", None, None, None),
        P("replica", "mp", None, None, None),
    )
    out_specs = (
        P(None, "mp", "replica"),
        P("replica", "mp", None, None, None),
        P("replica", "mp", None, None, None),
    )
    return jax.shard_map(body, mesh=mesh, in_specs=in_specs, out_specs=out_specs, check_vma=False)
```

```python
import functools
import math
import jax
import jax.numpy as jnp
from jax import lax
from jax.experimental import pallas as pl
from jax.experimental.pallas import tpu as pltpu
from jax.sharding import PartitionSpec as P

bf16 = jnp.bfloat16
f32 = jnp.float32
beta_first = 0.9
beta_second = 0.95
epsilon = 1e-08
decay_start = 9000.0
decay_length = 1000.0
MIB = 1024 * 1024
VMEM_LIMIT = 12 * MIB
TILE_VMEM = 24 * MIB
SMALL_VMEM = 4 * MIB
PIECES = 2


def plan_kernel(owners_ref, shifted_ref, tile_of_ref, slot_of_ref, held_ref):
    replica_id, my_index = lax.axis_index("replica"), lax.axis_index("mp")
    _, tile_cols, tile_rows = owners_ref.shape
    devices_mp = lax.axis_size("mp")
    counts = tile_of_ref.shape[0] - devices_mp
    capacity = counts // devices_mp
    for i in range(tile_of_ref.shape[0]):
        tile_of_ref[i] = 0

    def step(l, carry):
        for j in range(tile_cols):
            owner = owners_ref[replica_id, j, l]
            rank = tile_of_ref[counts + owner]
            tile_of_ref[counts + owner] = rank + 1
            slot = owner * capacity + rank
            tile_of_ref[slot] = l * tile_cols + j
            slot_of_ref[l * tile_cols + j] = slot
        return carry

    lax.fori_loop(0, tile_rows, step, 0)
    held_ref[0] = tile_of_ref[counts + my_index]
    held_ref[1] = shifted_ref[0, 0, 0] - owners_ref[0, 0, 0]


def make_plan(owners, shifted, devices_mp, capacity):
    tiles = owners.shape[1] * owners.shape[2]
    smem = pl.BlockSpec(memory_space=pltpu.SMEM)
    return pl.pallas_call(
        plan_kernel,
        out_shape=(
            jax.ShapeDtypeStruct((devices_mp * (capacity + 1),), jnp.int32),
            jax.ShapeDtypeStruct((tiles,), jnp.int32),
            jax.ShapeDtypeStruct((2,), jnp.int32),
        ),
        in_specs=[smem, smem],
        out_specs=(smem, smem, smem),
        compiler_params=pltpu.CompilerParams(vmem_limit_bytes=MIB),
        name="plan",
    )(owners, shifted)


def block_kernel(blocks, replicas, width, part_ref, *refs):
    replica_id = lax.axis_index("replica")
    *outs, sems = refs
    rows = part_ref.shape[0] // PIECES
    copies = []
    for k, (offset, start, size) in enumerate(blocks):
        column = lax.rem(replica_id + offset + replicas, replicas) * width + start
        for p in range(PIECES):
            some = slice(p * rows, (p + 1) * rows)
            source = part_ref.at[some, :, pl.ds(pl.multiple_of(column, 128), size)]
            copies.append(pltpu.make_async_copy(source, outs[k].at[some], sems.at[k, p]))
    for copy in copies:
        copy.start()
    for copy in copies:
        copy.wait()


def fetch_blocks(part, replicas, width, blocks, name):
    shapes = tuple(pltpu.VMEM(part.shape[:2] + (size,), part.dtype) for _, _, size in blocks)
    return pl.pallas_call(
        functools.partial(block_kernel, blocks, replicas, width),
        in_specs=[pl.BlockSpec(memory_space=pl.ANY)],
        out_specs=(pl.BlockSpec(memory_space=pltpu.VMEM),) * len(blocks),
        out_shape=shapes,
        scratch_shapes=[pltpu.SemaphoreType.DMA((len(blocks), PIECES))],
        compiler_params=pltpu.CompilerParams(vmem_limit_bytes=SMALL_VMEM),
        name=name,
    )(pltpu.with_memory_space_constraint(part, pltpu.HBM))


def add_kernel(start, block_ref, arrived_ref, out_ref):
    rows, _, width = block_ref.shape
    size = arrived_ref.shape[2]
    cols = slice(start, start + size)
    rest = slice(0, start) if start else slice(size, width)
    for l in range(rows):
        out_ref[l, :, cols] = block_ref[l, :, cols] + arrived_ref[l]
        if size < width:
            out_ref[l, :, rest] = block_ref[l, :, rest]


def add_block(block, arrived, start):
    vmem = pl.BlockSpec(memory_space=pltpu.VMEM)
    return pl.pallas_call(
        functools.partial(add_kernel, start),
        in_specs=[vmem, vmem],
        out_specs=vmem,
        out_shape=pltpu.VMEM(block.shape, block.dtype),
        compiler_params=pltpu.CompilerParams(vmem_limit_bytes=SMALL_VMEM),
        name="add_block",
    )(block, pltpu.with_memory_space_constraint(arrived, pltpu.VMEM))


def pack_kernel(tile_of_ref, own_ref, above_ref, below_ref, out_ref, sums_ref):
    tile_rows, sub_rows, width = own_ref.shape
    half = width // 2
    for l in range(tile_rows):
        total = (
            own_ref[l].astype(f32) + above_ref[l].astype(f32) + below_ref[l].astype(f32)
        ).astype(bf16)
        sums_ref[2 * l] = total[:, :half]
        sums_ref[2 * l + 1] = total[:, half:]
    devices_mp, capacity = out_ref.shape[:2]

    def step(m, carry):
        for c in range(capacity):
            out_ref[m, c] = sums_ref[tile_of_ref[m * capacity + c]]
        return carry

    lax.fori_loop(0, devices_mp, step, 0, unroll=4)


def pack(tile_of, own, above, below, devices_mp, capacity):
    tile_rows, sub_rows, width = own.shape
    vmem = pl.BlockSpec(memory_space=pltpu.VMEM)
    return pl.pallas_call(
        pack_kernel,
        in_specs=[pl.BlockSpec(memory_space=pltpu.SMEM), vmem, vmem, vmem],
        out_specs=vmem,
        out_shape=jax.ShapeDtypeStruct((devices_mp, capacity, sub_rows, width // 2), bf16),
        scratch_shapes=[pltpu.VMEM((2 * tile_rows, sub_rows, width // 2), bf16)],
        compiler_params=pltpu.CompilerParams(vmem_limit_bytes=VMEM_LIMIT),
        name="pack",
    )(tile_of, own, above, below)


def dot(a, b):
    return jnp.dot(a, b, preferred_element_type=f32)


def in_pieces(source, target, sems):
    slots, rows, _ = source.shape
    size = rows // PIECES
    return [
        pltpu.make_async_copy(
            source.at[s, pl.ds(p * size, size)], target.at[s, pl.ds(p * size, size)], sems.at[s, p]
        )
        for s in range(slots)
        for p in range(PIECES)
    ]


def prepare_kernel(
    left_hbm, right_hbm, first_hbm, second_hbm, left, left_t, right, right_t, first, second, sems
):
    pairs = ((left_hbm, left), (right_hbm, right), (first_hbm, first), (second_hbm, second))
    arrivals = [in_pieces(a, b, sems.at[k]) for k, (a, b) in enumerate(pairs)]
    for copies in arrivals:
        for copy in copies:
            copy.start()
    for k, copies in enumerate(arrivals):
        for copy in copies:
            copy.wait()
        if k < 2:
            source, target = ((left, left_t), (right, right_t))[k]
            for s in range(source.shape[0]):
                target[s] = source[s].T


def prepare(left, right, first, second):
    hbm = pl.BlockSpec(memory_space=pl.ANY)
    vmem = pl.BlockSpec(memory_space=pltpu.VMEM)
    square, wide = pltpu.VMEM(left.shape, bf16), pltpu.VMEM(left.shape, f32)
    return pl.pallas_call(
        prepare_kernel,
        in_specs=[hbm] * 4,
        out_specs=(vmem,) * 6,
        out_shape=(square, square, square, square, square, wide),
        scratch_shapes=[pltpu.SemaphoreType.DMA((4, left.shape[0], PIECES))],
        compiler_params=pltpu.CompilerParams(vmem_limit_bytes=SMALL_VMEM),
        name="prepare",
    )(*(pltpu.with_memory_space_constraint(a, pltpu.HBM) for a in (left, right, first, second)))


def tile_kernel(
    held_ref, grad, left, left_t, right, right_t, first, second,
    update, first_hbm, second_hbm, first_out, second_out, returned, sems,
):
    capacity, size, _ = left.shape
    devices_mp, _, sub_rows, _ = grad.shape
    half = size // 2
    step_value = jnp.full((8, 128), held_ref[1], jnp.int32).astype(f32)
    scale = -(1.0 - (step_value - decay_start) / decay_length)[:1, :1]
    first_fix = (1.0 / (1.0 - jnp.exp(step_value * math.log(beta_first))))[:1, :1]
    second_fix = (1.0 / (1.0 - jnp.exp(step_value * math.log(beta_second))))[:1, :1]

    def work(slots):
        projected = {
            s: dot(left_t[s], grad[:, s].reshape(size, size)).astype(bf16) for s in slots
        }
        for start in (0, half):
            cols = slice(start, start + half)
            for s in slots:
                rotated = dot(projected[s], right[s, :, cols])
                first_new = (
                    beta_first * first[s, :, cols].astype(f32) + (1.0 - beta_first) * rotated
                )
                second_new = (
                    beta_second * second[s, :, cols] + (1.0 - beta_second) * rotated * rotated
                )
                first_out[s, :, cols] = first_new.astype(bf16)
                second_out[s, :, cols] = second_new
                direction = (
                    first_new * first_fix / (jnp.sqrt(second_new * second_fix) + epsilon)
                ).astype(bf16)
                returned[s, :, cols] = dot(left[s], direction).astype(bf16)
        leave(slots)
        for s in slots:
            step = (scale * dot(returned[s], right_t[s])).astype(bf16)
            update[:, s] = step.reshape(devices_mp, sub_rows, size)

    def moments(s):
        return (
            pltpu.make_async_copy(second_out.at[s], second_hbm.at[s], sems.at[s, 0]),
            pltpu.make_async_copy(first_out.at[s], first_hbm.at[s], sems.at[s, 1]),
        )

    def leave(slots):
        for s in slots:
            for copy in moments(s):
                copy.start()

    def keep(slots):
        for s in slots:
            first_out[s] = first[s]
            second_out[s] = second[s]
            update[:, s] = jnp.zeros((devices_mp, sub_rows, size), bf16)
        leave(slots)

    for count in range(capacity + 1):

        @pl.when(held_ref[0] == count)
        def _():
            keep(range(count, capacity))
            work(range(count))

    for s in range(capacity):
        for copy in moments(s):
            copy.wait()


def tile_update(held, grads, ready):
    shape = ready[0].shape
    smem = pl.BlockSpec(memory_space=pltpu.SMEM)
    vmem = pl.BlockSpec(memory_space=pltpu.VMEM)
    hbm = pl.BlockSpec(memory_space=pl.ANY)
    return pl.pallas_call(
        tile_kernel,
        in_specs=[smem] + [vmem] * 7,
        out_specs=(vmem, hbm, hbm),
        out_shape=(
            pltpu.VMEM(grads.shape, bf16),
            jax.ShapeDtypeStruct(shape, bf16),
            jax.ShapeDtypeStruct(shape, f32),
        ),
        scratch_shapes=[
            pltpu.VMEM(shape, bf16),
            pltpu.VMEM(shape, f32),
            pltpu.VMEM(shape, bf16),
            pltpu.SemaphoreType.DMA((shape[0], 2)),
        ],
        compiler_params=pltpu.CompilerParams(vmem_limit_bytes=TILE_VMEM),
        name="tile_update",
    )(held, grads, *ready)


def place_kernel(slot_of_ref, back_ref, out_hbm, sems):
    tile_rows, sub_rows, width = out_hbm.shape
    _, _, size = back_ref.shape
    copies = [
        pltpu.make_async_copy(
            back_ref.at[slot_of_ref[t]],
            out_hbm.at[t * size // width, :, pl.ds(t * size % width, size)],
            sems.at[t],
        )
        for t in range(tile_rows * width // size)
    ]
    for copy in copies:
        copy.start()
    for copy in copies:
        copy.wait()


def place(slot_of, back, tile_rows):
    slots, sub_rows, size = back.shape
    return pl.pallas_call(
        place_kernel,
        in_specs=[
            pl.BlockSpec(memory_space=pltpu.SMEM),
            pl.BlockSpec(memory_space=pltpu.VMEM),
        ],
        out_specs=pl.BlockSpec(memory_space=pl.ANY),
        out_shape=jax.ShapeDtypeStruct((tile_rows, sub_rows, 2 * size), bf16),
        scratch_shapes=[pltpu.SemaphoreType.DMA((2 * tile_rows,))],
        compiler_params=pltpu.CompilerParams(vmem_limit_bytes=SMALL_VMEM),
        name="place",
    )(slot_of, back)


def together(*values):
    return lax.optimization_barrier(values)


def body(partials, owners, step_count, basis_left, basis_right, moment_first, moment_second):
    replicas = lax.axis_size("replica")
    devices_mp = lax.axis_size("mp")
    part, owners, shifted = together(
        partials[0], jnp.swapaxes(owners, 1, 2), jnp.swapaxes(owners + step_count, 1, 2)
    )
    tile_rows, sub_rows, columns = part.shape
    capacity = basis_left.shape[2]
    width = columns // replicas
    half = width // 2
    far = replicas // 2
    up = [(i, (i + 1) % replicas) for i in range(replicas)]
    down = [(i, (i - 1) % replicas) for i in range(replicas)]

    def swap(low, high):
        return lax.ppermute(low, "replica", down), lax.ppermute(high, "replica", up)

    first = ((far, 0, half), (far, half, half))
    low, high = fetch_blocks(part, replicas, width, first, "first_blocks")
    above, below = swap(low, high)
    low, part = together(low, part)
    order = [(sign * hops, 0, width) for hops in range(far - 1, 0, -1) for sign in (-1, 1)]
    rest = (*order, (0, 0, width))
    *blocks, own = fetch_blocks(part, replicas, width, rest, "rest_blocks")
    state = (owners, shifted, basis_left[0, 0], basis_right[0, 0], moment_first[0, 0], moment_second[0, 0])
    for hops in range(far - 1, 0, -1):
        low, high, *blocks = blocks
        low = add_block(low, above, 0)
        high = add_block(high, below, half if hops == far - 1 else 0)
        low, state = together(low, state)
        above, below = swap(low, high)
        if hops == far - 1:
            owners, shifted, *operands = state
            state = (make_plan(owners, shifted, devices_mp, capacity), operands)
        elif hops == far - 2:
            plan, operands = state
            state = (plan, prepare(*operands))
    (tile_of, slot_of, held), ready = state
    outgoing = pack(tile_of, own, above, below, devices_mp, capacity)
    arrived = lax.all_to_all(outgoing, "mp", split_axis=0, concat_axis=0, tiled=True)
    update, first_out, second_out = tile_update(held, arrived, ready)
    back = lax.all_to_all(update, "mp", split_axis=0, concat_axis=0, tiled=True)
    back = back.reshape(devices_mp * capacity, sub_rows, half)
    slab = place(slot_of, back, tile_rows)
    return slab, first_out[None, None], second_out[None, None]


def solution(mesh):
    in_specs = (
        P("replica", None, "mp", None),
        P(),
        P(),
        P("replica", "mp", None, None, None),
        P("replica", "mp", None, None, None),
        P("replica", "mp", None, None, None),
        P("replica", "mp", None, None, None),
    )
    out_specs = (
        P(None, "mp", "replica"),
        P("replica", "mp", None, None, None),
        P("replica", "mp", None, None, None),
    )
    return jax.shard_map(body, mesh=mesh, in_specs=in_specs, out_specs=out_specs, check_vma=False)
```

```python
import functools
import math
import jax
import jax.numpy as jnp
from jax import lax
from jax.experimental import pallas as pl
from jax.experimental.pallas import tpu as pltpu
from jax.sharding import PartitionSpec as P

bf16 = jnp.bfloat16
f32 = jnp.float32
beta_first = 0.9
beta_second = 0.95
epsilon = 1e-08
decay_start = 9000.0
decay_length = 1000.0
MIB = 1024 * 1024
VMEM_LIMIT = 12 * MIB
TILE_VMEM = 24 * MIB
SMALL_VMEM = 4 * MIB
PIECES = 2
RINGS = 2


def plan_kernel(owners_ref, shifted_ref, tile_of_ref, slot_of_ref, held_ref):
    replica_id, my_index = lax.axis_index("replica"), lax.axis_index("mp")
    _, tile_cols, tile_rows = owners_ref.shape
    devices_mp = lax.axis_size("mp")
    counts = tile_of_ref.shape[0] - devices_mp
    capacity = counts // devices_mp
    for i in range(tile_of_ref.shape[0]):
        tile_of_ref[i] = 0

    def step(l, carry):
        for j in range(tile_cols):
            owner = owners_ref[replica_id, j, l]
            rank = tile_of_ref[counts + owner]
            tile_of_ref[counts + owner] = rank + 1
            slot = owner * capacity + rank
            tile_of_ref[slot] = l * tile_cols + j
            slot_of_ref[l * tile_cols + j] = slot
        return carry

    lax.fori_loop(0, tile_rows, step, 0)
    held_ref[0] = tile_of_ref[counts + my_index]
    held_ref[1] = shifted_ref[0, 0, 0] - owners_ref[0, 0, 0]


def make_plan(owners, shifted, devices_mp, capacity):
    tiles = owners.shape[1] * owners.shape[2]
    smem = pl.BlockSpec(memory_space=pltpu.SMEM)
    return pl.pallas_call(
        plan_kernel,
        out_shape=(
            jax.ShapeDtypeStruct((devices_mp * (capacity + 1),), jnp.int32),
            jax.ShapeDtypeStruct((tiles,), jnp.int32),
            jax.ShapeDtypeStruct((2,), jnp.int32),
        ),
        in_specs=[smem, smem],
        out_specs=(smem, smem, smem),
        compiler_params=pltpu.CompilerParams(vmem_limit_bytes=MIB),
        name="plan",
    )(owners, shifted)


def block_kernel(blocks, replicas, width, part_ref, *refs):
    replica_id = lax.axis_index("replica")
    *outs, sems = refs
    copies = []
    for k, (pipe, offset, start, size) in enumerate(blocks):
        column = lax.rem(replica_id + offset + replicas, replicas) * width + start
        rows = outs[k].shape[0]
        source = part_ref.at[
            pl.ds(pipe * rows, rows), :, pl.ds(pl.multiple_of(column, 128), size)
        ]
        copies.append(pltpu.make_async_copy(source, outs[k], sems.at[k]))
    for copy in copies:
        copy.start()
    for copy in copies:
        copy.wait()


def fetch_blocks(part, replicas, width, blocks, name):
    rows = part.shape[0] // RINGS
    shapes = tuple(pltpu.VMEM((rows, part.shape[1], size), part.dtype) for *_, size in blocks)
    return pl.pallas_call(
        functools.partial(block_kernel, blocks, replicas, width),
        in_specs=[pl.BlockSpec(memory_space=pl.ANY)],
        out_specs=(pl.BlockSpec(memory_space=pltpu.VMEM),) * len(blocks),
        out_shape=shapes,
        scratch_shapes=[pltpu.SemaphoreType.DMA((len(blocks),))],
        compiler_params=pltpu.CompilerParams(vmem_limit_bytes=SMALL_VMEM),
        name=name,
    )(pltpu.with_memory_space_constraint(part, pltpu.HBM))


def add_kernel(start, block_ref, arrived_ref, out_ref):
    rows, _, width = block_ref.shape
    size = arrived_ref.shape[2]
    cols = slice(start, start + size)
    rest = slice(0, start) if start else slice(size, width)
    for l in range(rows):
        out_ref[l, :, cols] = block_ref[l, :, cols] + arrived_ref[l]
        if size < width:
            out_ref[l, :, rest] = block_ref[l, :, rest]


def add_block(block, arrived, start):
    vmem = pl.BlockSpec(memory_space=pltpu.VMEM)
    return pl.pallas_call(
        functools.partial(add_kernel, start),
        in_specs=[vmem, vmem],
        out_specs=vmem,
        out_shape=pltpu.VMEM(block.shape, block.dtype),
        compiler_params=pltpu.CompilerParams(vmem_limit_bytes=SMALL_VMEM),
        name="add_block",
    )(block, pltpu.with_memory_space_constraint(arrived, pltpu.VMEM))


def pack_kernel(tile_of_ref, *refs):
    *parts, out_ref, sums_ref = refs
    rows, sub_rows, width = parts[0].shape
    half = width // 2
    for ring in range(RINGS):
        own, above, below = parts[3 * ring : 3 * ring + 3]
        for l in range(rows):
            total = own[l].astype(f32) + above[l].astype(f32) + below[l].astype(f32)
            total = total.astype(bf16)
            tile = 2 * (ring * rows + l)
            sums_ref[tile] = total[:, :half]
            sums_ref[tile + 1] = total[:, half:]
    devices_mp, capacity = out_ref.shape[:2]

    def step(m, carry):
        for c in range(capacity):
            out_ref[m, c] = sums_ref[tile_of_ref[m * capacity + c]]
        return carry

    lax.fori_loop(0, devices_mp, step, 0, unroll=4)


def pack(tile_of, parts, devices_mp, capacity):
    rows, sub_rows, width = parts[0].shape
    vmem = pl.BlockSpec(memory_space=pltpu.VMEM)
    return pl.pallas_call(
        pack_kernel,
        in_specs=[pl.BlockSpec(memory_space=pltpu.SMEM)] + [vmem] * len(parts),
        out_specs=vmem,
        out_shape=jax.ShapeDtypeStruct((devices_mp, capacity, sub_rows, width // 2), bf16),
        scratch_shapes=[pltpu.VMEM((2 * RINGS * rows, sub_rows, width // 2), bf16)],
        compiler_params=pltpu.CompilerParams(vmem_limit_bytes=VMEM_LIMIT),
        name="pack",
    )(tile_of, *parts)


def dot(a, b):
    return jnp.dot(a, b, preferred_element_type=f32)


def in_pieces(source, target, sems):
    slots, rows, _ = source.shape
    size = rows // PIECES
    return [
        pltpu.make_async_copy(
            source.at[s, pl.ds(p * size, size)], target.at[s, pl.ds(p * size, size)], sems.at[s, p]
        )
        for s in range(slots)
        for p in range(PIECES)
    ]


def prepare_kernel(
    left_hbm, right_hbm, first_hbm, second_hbm, left, left_t, right, right_t, first, second, sems
):
    pairs = ((left_hbm, left), (right_hbm, right), (first_hbm, first), (second_hbm, second))
    arrivals = [in_pieces(a, b, sems.at[k]) for k, (a, b) in enumerate(pairs)]
    for copies in arrivals:
        for copy in copies:
            copy.start()
    for k, copies in enumerate(arrivals):
        for copy in copies:
            copy.wait()
        if k < 2:
            source, target = ((left, left_t), (right, right_t))[k]
            for s in range(source.shape[0]):
                target[s] = source[s].T


def prepare(left, right, first, second):
    hbm = pl.BlockSpec(memory_space=pl.ANY)
    vmem = pl.BlockSpec(memory_space=pltpu.VMEM)
    square, wide = pltpu.VMEM(left.shape, bf16), pltpu.VMEM(left.shape, f32)
    return pl.pallas_call(
        prepare_kernel,
        in_specs=[hbm] * 4,
        out_specs=(vmem,) * 6,
        out_shape=(square, square, square, square, square, wide),
        scratch_shapes=[pltpu.SemaphoreType.DMA((4, left.shape[0], PIECES))],
        compiler_params=pltpu.CompilerParams(vmem_limit_bytes=SMALL_VMEM),
        name="prepare",
    )(*(pltpu.with_memory_space_constraint(a, pltpu.HBM) for a in (left, right, first, second)))


def tile_kernel(
    held_ref, grad, left, left_t, right, right_t, first, second,
    update, first_hbm, second_hbm, first_out, second_out, returned, sems,
):
    capacity, size, _ = left.shape
    devices_mp, _, sub_rows, _ = grad.shape
    half = size // 2
    step_value = jnp.full((8, 128), held_ref[1], jnp.int32).astype(f32)
    scale = -(1.0 - (step_value - decay_start) / decay_length)[:1, :1]
    first_fix = (1.0 / (1.0 - jnp.exp(step_value * math.log(beta_first))))[:1, :1]
    second_fix = (1.0 / (1.0 - jnp.exp(step_value * math.log(beta_second))))[:1, :1]

    def work(slots):
        projected = {
            s: dot(left_t[s], grad[:, s].reshape(size, size)).astype(bf16) for s in slots
        }
        for start in (0, half):
            cols = slice(start, start + half)
            for s in slots:
                rotated = dot(projected[s], right[s, :, cols])
                first_new = (
                    beta_first * first[s, :, cols].astype(f32) + (1.0 - beta_first) * rotated
                )
                second_new = (
                    beta_second * second[s, :, cols] + (1.0 - beta_second) * rotated * rotated
                )
                first_out[s, :, cols] = first_new.astype(bf16)
                second_out[s, :, cols] = second_new
                direction = (
                    first_new * first_fix / (jnp.sqrt(second_new * second_fix) + epsilon)
                ).astype(bf16)
                returned[s, :, cols] = dot(left[s], direction).astype(bf16)
        leave(slots)
        for s in slots:
            step = (scale * dot(returned[s], right_t[s])).astype(bf16)
            update[:, s] = step.reshape(devices_mp, sub_rows, size)

    def moments(s):
        return (
            pltpu.make_async_copy(second_out.at[s], second_hbm.at[s], sems.at[s, 0]),
            pltpu.make_async_copy(first_out.at[s], first_hbm.at[s], sems.at[s, 1]),
        )

    def leave(slots):
        for s in slots:
            for copy in moments(s):
                copy.start()

    def keep(slots):
        for s in slots:
            first_out[s] = first[s]
            second_out[s] = second[s]
            update[:, s] = jnp.zeros((devices_mp, sub_rows, size), bf16)
        leave(slots)

    for count in range(capacity + 1):

        @pl.when(held_ref[0] == count)
        def _():
            keep(range(count, capacity))
            work(range(count))

    for s in range(capacity):
        for copy in moments(s):
            copy.wait()


def tile_update(held, grads, ready):
    shape = ready[0].shape
    smem = pl.BlockSpec(memory_space=pltpu.SMEM)
    vmem = pl.BlockSpec(memory_space=pltpu.VMEM)
    hbm = pl.BlockSpec(memory_space=pl.ANY)
    return pl.pallas_call(
        tile_kernel,
        in_specs=[smem] + [vmem] * 7,
        out_specs=(vmem, hbm, hbm),
        out_shape=(
            pltpu.VMEM(grads.shape, bf16),
            jax.ShapeDtypeStruct(shape, bf16),
            jax.ShapeDtypeStruct(shape, f32),
        ),
        scratch_shapes=[
            pltpu.VMEM(shape, bf16),
            pltpu.VMEM(shape, f32),
            pltpu.VMEM(shape, bf16),
            pltpu.SemaphoreType.DMA((shape[0], 2)),
        ],
        compiler_params=pltpu.CompilerParams(vmem_limit_bytes=TILE_VMEM),
        name="tile_update",
    )(held, grads, *ready)


def place_kernel(slot_of_ref, back_ref, out_hbm, sems):
    tile_rows, sub_rows, width = out_hbm.shape
    _, _, size = back_ref.shape
    copies = [
        pltpu.make_async_copy(
            back_ref.at[slot_of_ref[t]],
            out_hbm.at[t * size // width, :, pl.ds(t * size % width, size)],
            sems.at[t],
        )
        for t in range(tile_rows * width // size)
    ]
    for copy in copies:
        copy.start()
    for copy in copies:
        copy.wait()


def place(slot_of, back, tile_rows):
    slots, sub_rows, size = back.shape
    return pl.pallas_call(
        place_kernel,
        in_specs=[
            pl.BlockSpec(memory_space=pltpu.SMEM),
            pl.BlockSpec(memory_space=pltpu.VMEM),
        ],
        out_specs=pl.BlockSpec(memory_space=pl.ANY),
        out_shape=jax.ShapeDtypeStruct((tile_rows, sub_rows, 2 * size), bf16),
        scratch_shapes=[pltpu.SemaphoreType.DMA((2 * tile_rows,))],
        compiler_params=pltpu.CompilerParams(vmem_limit_bytes=SMALL_VMEM),
        name="place",
    )(slot_of, back)


def together(*values):
    return lax.optimization_barrier(values)


def body(partials, owners, step_count, basis_left, basis_right, moment_first, moment_second):
    replicas = lax.axis_size("replica")
    devices_mp = lax.axis_size("mp")
    part, owners, shifted = together(
        partials[0], jnp.swapaxes(owners, 1, 2), jnp.swapaxes(owners + step_count, 1, 2)
    )
    tile_rows, sub_rows, columns = part.shape
    capacity = basis_left.shape[2]
    width = columns // replicas
    half = width // 2
    far = replicas // 2
    up = [(i, (i + 1) % replicas) for i in range(replicas)]
    down = [(i, (i - 1) % replicas) for i in range(replicas)]

    def swap(low, high):
        return lax.ppermute(low, "replica", down), lax.ppermute(high, "replica", up)

    rings = range(RINGS)
    first = [(ring, far, start, half) for ring in rings for start in (0, half)]
    firsts = fetch_blocks(part, replicas, width, first, "first_blocks")
    moving = [swap(firsts[2 * ring], firsts[2 * ring + 1]) for ring in rings]
    _, part = together(firsts[0], part)
    rest = [
        (ring, sign * hops, 0, width)
        for hops in range(far - 1, 0, -1)
        for ring in rings
        for sign in (-1, 1)
    ]
    rest += [(ring, 0, 0, width) for ring in rings]
    blocks = list(fetch_blocks(part, replicas, width, rest, "rest_blocks"))
    owns = blocks[-RINGS:]
    state = (
        owners, shifted, basis_left[0, 0], basis_right[0, 0], moment_first[0, 0], moment_second[0, 0]
    )
    for hops in range(far - 1, 0, -1):
        for ring in rings:
            above, below = moving[ring]
            low = add_block(blocks.pop(0), above, 0)
            high = add_block(blocks.pop(0), below, half if hops == far - 1 else 0)
            if ring == RINGS - 1:
                low, state = together(low, state)
            moving[ring] = swap(low, high)
        if hops == far - 1:
            owners, shifted, *operands = state
            state = (make_plan(owners, shifted, devices_mp, capacity), operands)
        elif hops == far - 2:
            plan, operands = state
            state = (plan, prepare(*operands))
    (tile_of, slot_of, held), ready = state
    parts = [x for ring in rings for x in (owns[ring], *moving[ring])]
    outgoing = pack(tile_of, parts, devices_mp, capacity)
    arrived = lax.all_to_all(outgoing, "mp", split_axis=0, concat_axis=0, tiled=True)
    update, first_out, second_out = tile_update(held, arrived, ready)
    back = lax.all_to_all(update, "mp", split_axis=0, concat_axis=0, tiled=True)
    back = back.reshape(devices_mp * capacity, sub_rows, half)
    slab = place(slot_of, back, tile_rows)
    return slab, first_out[None, None], second_out[None, None]


def solution(mesh):
    in_specs = (
        P("replica", None, "mp", None),
        P(),
        P(),
        P("replica", "mp", None, None, None),
        P("replica", "mp", None, None, None),
        P("replica", "mp", None, None, None),
        P("replica", "mp", None, None, None),
    )
    out_specs = (
        P(None, "mp", "replica"),
        P("replica", "mp", None, None, None),
        P("replica", "mp", None, None, None),
    )
    return jax.shard_map(body, mesh=mesh, in_specs=in_specs, out_specs=out_specs, check_vma=False)
```

```python
import functools
import math
import jax
import jax.numpy as jnp
from jax import lax
from jax.experimental import pallas as pl
from jax.experimental.pallas import tpu as pltpu
from jax.sharding import PartitionSpec as P

bf16 = jnp.bfloat16
f32 = jnp.float32
beta_first = 0.9
beta_second = 0.95
epsilon = 1e-08
decay_start = 9000.0
decay_length = 1000.0
MIB = 1024 * 1024
VMEM_LIMIT = 12 * MIB
TILE_VMEM = 24 * MIB
SMALL_VMEM = 4 * MIB
PIECES = 2
RINGS = 2


def plan_kernel(owners_ref, shifted_ref, tile_of_ref, slot_of_ref, held_ref):
    replica_id, my_index = lax.axis_index("replica"), lax.axis_index("mp")
    _, tile_cols, tile_rows = owners_ref.shape
    devices_mp = lax.axis_size("mp")
    counts = tile_of_ref.shape[0] - devices_mp
    capacity = counts // devices_mp
    for i in range(tile_of_ref.shape[0]):
        tile_of_ref[i] = 0

    def step(l, carry):
        for j in range(tile_cols):
            owner = owners_ref[replica_id, j, l]
            rank = tile_of_ref[counts + owner]
            tile_of_ref[counts + owner] = rank + 1
            slot = owner * capacity + rank
            tile_of_ref[slot] = l * tile_cols + j
            slot_of_ref[l * tile_cols + j] = slot
        return carry

    lax.fori_loop(0, tile_rows, step, 0)
    held_ref[0] = tile_of_ref[counts + my_index]
    held_ref[1] = shifted_ref[0, 0, 0] - owners_ref[0, 0, 0]


def make_plan(owners, shifted, devices_mp, capacity):
    tiles = owners.shape[1] * owners.shape[2]
    smem = pl.BlockSpec(memory_space=pltpu.SMEM)
    return pl.pallas_call(
        plan_kernel,
        out_shape=(
            jax.ShapeDtypeStruct((devices_mp * (capacity + 1),), jnp.int32),
            jax.ShapeDtypeStruct((tiles,), jnp.int32),
            jax.ShapeDtypeStruct((2,), jnp.int32),
        ),
        in_specs=[smem, smem],
        out_specs=(smem, smem, smem),
        compiler_params=pltpu.CompilerParams(vmem_limit_bytes=MIB),
        name="plan",
    )(owners, shifted)


def block_kernel(blocks, replicas, width, part_ref, *refs):
    replica_id = lax.axis_index("replica")
    *outs, sems = refs
    copies = []
    for k, (pipe, offset, start, size) in enumerate(blocks):
        column = lax.rem(replica_id + offset + replicas, replicas) * width + start
        rows = outs[k].shape[0]
        source = part_ref.at[
            pl.ds(pipe * rows, rows), :, pl.ds(pl.multiple_of(column, 128), size)
        ]
        copies.append(pltpu.make_async_copy(source, outs[k], sems.at[k]))
    for copy in copies:
        copy.start()
    for copy in copies:
        copy.wait()


def fetch_blocks(part, replicas, width, blocks, name):
    rows = part.shape[0] // RINGS
    shapes = tuple(pltpu.VMEM((rows, part.shape[1], size), part.dtype) for *_, size in blocks)
    return pl.pallas_call(
        functools.partial(block_kernel, blocks, replicas, width),
        in_specs=[pl.BlockSpec(memory_space=pl.ANY)],
        out_specs=(pl.BlockSpec(memory_space=pltpu.VMEM),) * len(blocks),
        out_shape=shapes,
        scratch_shapes=[pltpu.SemaphoreType.DMA((len(blocks),))],
        compiler_params=pltpu.CompilerParams(vmem_limit_bytes=SMALL_VMEM),
        name=name,
    )(pltpu.with_memory_space_constraint(part, pltpu.HBM))


def add_kernel(start, block_ref, arrived_ref, out_ref):
    rows, _, width = block_ref.shape
    size = arrived_ref.shape[2]
    cols = slice(start, start + size)
    rest = slice(0, start) if start else slice(size, width)
    for l in range(rows):
        out_ref[l, :, cols] = block_ref[l, :, cols] + arrived_ref[l]
        if size < width:
            out_ref[l, :, rest] = block_ref[l, :, rest]


def add_block(block, arrived, start):
    vmem = pl.BlockSpec(memory_space=pltpu.VMEM)
    return pl.pallas_call(
        functools.partial(add_kernel, start),
        in_specs=[vmem, vmem],
        out_specs=vmem,
        out_shape=pltpu.VMEM(block.shape, block.dtype),
        compiler_params=pltpu.CompilerParams(vmem_limit_bytes=SMALL_VMEM),
        name="add_block",
    )(block, pltpu.with_memory_space_constraint(arrived, pltpu.VMEM))


def pack_kernel(tile_of_ref, *refs):
    *parts, out_ref, sums_ref = refs
    rows, sub_rows, width = parts[0].shape
    half = width // 2
    for ring in range(RINGS):
        own, above, below = parts[3 * ring : 3 * ring + 3]
        for l in range(rows):
            total = own[l].astype(f32) + above[l].astype(f32) + below[l].astype(f32)
            total = total.astype(bf16)
            tile = 2 * (ring * rows + l)
            sums_ref[tile] = total[:, :half]
            sums_ref[tile + 1] = total[:, half:]
    devices_mp, capacity = out_ref.shape[:2]

    def step(m, carry):
        for c in range(capacity):
            out_ref[m, c] = sums_ref[tile_of_ref[m * capacity + c]]
        return carry

    lax.fori_loop(0, devices_mp, step, 0, unroll=4)


def pack(tile_of, parts, devices_mp, capacity):
    rows, sub_rows, width = parts[0].shape
    vmem = pl.BlockSpec(memory_space=pltpu.VMEM)
    return pl.pallas_call(
        pack_kernel,
        in_specs=[pl.BlockSpec(memory_space=pltpu.SMEM)] + [vmem] * len(parts),
        out_specs=vmem,
        out_shape=jax.ShapeDtypeStruct((devices_mp, capacity, sub_rows, width // 2), bf16),
        scratch_shapes=[pltpu.VMEM((2 * RINGS * rows, sub_rows, width // 2), bf16)],
        compiler_params=pltpu.CompilerParams(vmem_limit_bytes=VMEM_LIMIT),
        name="pack",
    )(tile_of, *parts)


def dot(a, b):
    return jnp.dot(a, b, preferred_element_type=f32)


def in_pieces(source, target, sems):
    slots, rows, _ = source.shape
    size = rows // PIECES
    return [
        pltpu.make_async_copy(
            source.at[s, pl.ds(p * size, size)], target.at[s, pl.ds(p * size, size)], sems.at[s, p]
        )
        for s in range(slots)
        for p in range(PIECES)
    ]


def prepare_kernel(
    left_hbm, right_hbm, first_hbm, second_hbm, left, left_t, right, right_t, first, second, sems
):
    pairs = ((left_hbm, left), (right_hbm, right), (first_hbm, first), (second_hbm, second))
    arrivals = [in_pieces(a, b, sems.at[k]) for k, (a, b) in enumerate(pairs)]
    for copies in arrivals:
        for copy in copies:
            copy.start()
    for k, copies in enumerate(arrivals):
        for copy in copies:
            copy.wait()
        if k < 2:
            source, target = ((left, left_t), (right, right_t))[k]
            for s in range(source.shape[0]):
                target[s] = source[s].T


def prepare(left, right, first, second):
    hbm = pl.BlockSpec(memory_space=pl.ANY)
    vmem = pl.BlockSpec(memory_space=pltpu.VMEM)
    square, wide = pltpu.VMEM(left.shape, bf16), pltpu.VMEM(left.shape, f32)
    return pl.pallas_call(
        prepare_kernel,
        in_specs=[hbm] * 4,
        out_specs=(vmem,) * 6,
        out_shape=(square, square, square, square, square, wide),
        scratch_shapes=[pltpu.SemaphoreType.DMA((4, left.shape[0], PIECES))],
        compiler_params=pltpu.CompilerParams(vmem_limit_bytes=SMALL_VMEM),
        name="prepare",
    )(*(pltpu.with_memory_space_constraint(a, pltpu.HBM) for a in (left, right, first, second)))


def tile_kernel(
    held_ref, grad, left, left_t, right, right_t, first, second,
    update, first_hbm, second_hbm, first_out, second_out, returned, sems,
):
    capacity, size, _ = left.shape
    devices_mp, _, sub_rows, _ = grad.shape
    half = size // 2
    step_value = jnp.full((8, 128), held_ref[1], jnp.int32).astype(f32)
    scale = -(1.0 - (step_value - decay_start) / decay_length)[:1, :1]
    first_fix = (1.0 / (1.0 - jnp.exp(step_value * math.log(beta_first))))[:1, :1]
    second_fix = (1.0 / (1.0 - jnp.exp(step_value * math.log(beta_second))))[:1, :1]

    def work(slots):
        projected = {
            s: dot(left_t[s], grad[:, s].reshape(size, size)).astype(bf16) for s in slots
        }
        for start in (0, half):
            cols = slice(start, start + half)
            for s in slots:
                rotated = dot(projected[s], right[s, :, cols])
                first_new = (
                    beta_first * first[s, :, cols].astype(f32) + (1.0 - beta_first) * rotated
                )
                second_new = (
                    beta_second * second[s, :, cols] + (1.0 - beta_second) * rotated * rotated
                )
                first_out[s, :, cols] = first_new.astype(bf16)
                second_out[s, :, cols] = second_new
                direction = (
                    first_new * first_fix / (jnp.sqrt(second_new * second_fix) + epsilon)
                ).astype(bf16)
                returned[s, :, cols] = dot(left[s], direction).astype(bf16)
        leave(slots)
        for s in slots:
            step = (scale * dot(returned[s], right_t[s])).astype(bf16)
            update[:, s] = step.reshape(devices_mp, sub_rows, size)

    def moments(s):
        return (
            pltpu.make_async_copy(second_out.at[s], second_hbm.at[s], sems.at[s, 0]),
            pltpu.make_async_copy(first_out.at[s], first_hbm.at[s], sems.at[s, 1]),
        )

    def leave(slots):
        for s in slots:
            for copy in moments(s):
                copy.start()

    def keep(slots):
        for s in slots:
            first_out[s] = first[s]
            second_out[s] = second[s]
            update[:, s] = jnp.zeros((devices_mp, sub_rows, size), bf16)
        leave(slots)

    for count in range(capacity + 1):

        @pl.when(held_ref[0] == count)
        def _():
            keep(range(count, capacity))
            work(range(count))

    for s in range(capacity):
        for copy in moments(s):
            copy.wait()


def tile_update(held, grads, ready):
    shape = ready[0].shape
    smem = pl.BlockSpec(memory_space=pltpu.SMEM)
    vmem = pl.BlockSpec(memory_space=pltpu.VMEM)
    hbm = pl.BlockSpec(memory_space=pl.ANY)
    return pl.pallas_call(
        tile_kernel,
        in_specs=[smem] + [vmem] * 7,
        out_specs=(vmem, hbm, hbm),
        out_shape=(
            pltpu.VMEM(grads.shape, bf16),
            jax.ShapeDtypeStruct(shape, bf16),
            jax.ShapeDtypeStruct(shape, f32),
        ),
        scratch_shapes=[
            pltpu.VMEM(shape, bf16),
            pltpu.VMEM(shape, f32),
            pltpu.VMEM(shape, bf16),
            pltpu.SemaphoreType.DMA((shape[0], 2)),
        ],
        compiler_params=pltpu.CompilerParams(vmem_limit_bytes=TILE_VMEM),
        name="tile_update",
    )(held, grads, *ready)


def place_kernel(slot_of_ref, back_ref, out_hbm, sems):
    tile_rows, sub_rows, width = out_hbm.shape
    _, _, size = back_ref.shape
    copies = [
        pltpu.make_async_copy(
            back_ref.at[slot_of_ref[t]],
            out_hbm.at[t * size // width, :, pl.ds(t * size % width, size)],
            sems.at[t],
        )
        for t in range(tile_rows * width // size)
    ]
    for copy in copies:
        copy.start()
    for copy in copies:
        copy.wait()


def place(slot_of, back, tile_rows):
    slots, sub_rows, size = back.shape
    return pl.pallas_call(
        place_kernel,
        in_specs=[
            pl.BlockSpec(memory_space=pltpu.SMEM),
            pl.BlockSpec(memory_space=pltpu.VMEM),
        ],
        out_specs=pl.BlockSpec(memory_space=pl.ANY),
        out_shape=jax.ShapeDtypeStruct((tile_rows, sub_rows, 2 * size), bf16),
        scratch_shapes=[pltpu.SemaphoreType.DMA((2 * tile_rows,))],
        compiler_params=pltpu.CompilerParams(vmem_limit_bytes=SMALL_VMEM),
        name="place",
    )(slot_of, back)


def together(*values):
    return lax.optimization_barrier(values)


def body(partials, owners, step_count, basis_left, basis_right, moment_first, moment_second):
    replicas = lax.axis_size("replica")
    devices_mp = lax.axis_size("mp")
    part, owners, shifted = together(
        partials[0], jnp.swapaxes(owners, 1, 2), jnp.swapaxes(owners + step_count, 1, 2)
    )
    tile_rows, sub_rows, columns = part.shape
    capacity = basis_left.shape[2]
    width = columns // replicas
    half = width // 2
    far = replicas // 2
    up = [(i, (i + 1) % replicas) for i in range(replicas)]
    down = [(i, (i - 1) % replicas) for i in range(replicas)]

    def swap(low, high):
        return lax.ppermute(low, "replica", down), lax.ppermute(high, "replica", up)

    rings = range(RINGS)
    first = [(ring, far, start, half) for ring in rings for start in (0, half)]
    firsts = fetch_blocks(part, replicas, width, first, "first_blocks")
    moving = [swap(firsts[2 * ring], firsts[2 * ring + 1]) for ring in rings]
    _, part = together(firsts[0], part)
    rest = [
        (ring, sign * hops, 0, width)
        for hops in range(far - 1, 0, -1)
        for ring in rings
        for sign in (-1, 1)
    ]
    rest += [(ring, 0, 0, width) for ring in rings]
    blocks = list(fetch_blocks(part, replicas, width, rest, "rest_blocks"))
    owns = blocks[-RINGS:]
    state = (
        owners, shifted, basis_left[0, 0], basis_right[0, 0], moment_first[0, 0], moment_second[0, 0]
    )
    for hops in range(far - 1, 0, -1):
        for ring in rings:
            above, below = moving[ring]
            low = add_block(blocks.pop(0), above, 0)
            high = add_block(blocks.pop(0), below, half if hops == far - 1 else 0)
            if ring == RINGS - 1:
                low, state = together(low, state)
            moving[ring] = swap(low, high)
        if hops == far - 1:
            owners, shifted, *operands = state
            state = (make_plan(owners, shifted, devices_mp, capacity), operands)
    plan, operands = state
    moving, plan, ready = together(moving, plan, prepare(*operands))
    tile_of, slot_of, held = plan
    parts = [x for ring in rings for x in (owns[ring], *moving[ring])]
    outgoing = pack(tile_of, parts, devices_mp, capacity)
    arrived = lax.all_to_all(outgoing, "mp", split_axis=0, concat_axis=0, tiled=True)
    update, first_out, second_out = tile_update(held, arrived, ready)
    back = lax.all_to_all(update, "mp", split_axis=0, concat_axis=0, tiled=True)
    back = back.reshape(devices_mp * capacity, sub_rows, half)
    slab = place(slot_of, back, tile_rows)
    return slab, first_out[None, None], second_out[None, None]


def solution(mesh):
    in_specs = (
        P("replica", None, "mp", None),
        P(),
        P(),
        P("replica", "mp", None, None, None),
        P("replica", "mp", None, None, None),
        P("replica", "mp", None, None, None),
        P("replica", "mp", None, None, None),
    )
    out_specs = (
        P(None, "mp", "replica"),
        P("replica", "mp", None, None, None),
        P("replica", "mp", None, None, None),
    )
    return jax.shard_map(body, mesh=mesh, in_specs=in_specs, out_specs=out_specs, check_vma=False)
```

```python
import functools
import math
import jax
import jax.numpy as jnp
from jax import lax
from jax.experimental import pallas as pl
from jax.experimental.pallas import tpu as pltpu
from jax.sharding import PartitionSpec as P

bf16 = jnp.bfloat16
f32 = jnp.float32
beta_first = 0.9
beta_second = 0.95
epsilon = 1e-08
decay_start = 9000.0
decay_length = 1000.0
MIB = 1024 * 1024
VMEM_LIMIT = 12 * MIB
TILE_VMEM = 24 * MIB
SMALL_VMEM = 4 * MIB
PIECES = 2
RINGS = 2


def plan_kernel(owners_ref, step_ref, tile_of_ref, slot_of_ref, held_ref):
    replica_id, my_index = lax.axis_index("replica"), lax.axis_index("mp")
    _, tile_cols, tile_rows = owners_ref.shape
    devices_mp = lax.axis_size("mp")
    counts = tile_of_ref.shape[0] - devices_mp
    capacity = counts // devices_mp
    for i in range(tile_of_ref.shape[0]):
        tile_of_ref[i] = 0

    def step(l, carry):
        for j in range(tile_cols):
            owner = owners_ref[replica_id, j, l]
            rank = tile_of_ref[counts + owner]
            tile_of_ref[counts + owner] = rank + 1
            slot = owner * capacity + rank
            tile_of_ref[slot] = l * tile_cols + j
            slot_of_ref[l * tile_cols + j] = slot
        return carry

    lax.fori_loop(0, tile_rows, step, 0)
    held_ref[0] = tile_of_ref[counts + my_index]
    held_ref[1] = step_ref[0]


def make_plan(owners, steps, devices_mp, capacity):
    tiles = owners.shape[1] * owners.shape[2]
    smem = pl.BlockSpec(memory_space=pltpu.SMEM)
    return pl.pallas_call(
        plan_kernel,
        out_shape=(
            jax.ShapeDtypeStruct((devices_mp * (capacity + 1),), jnp.int32),
            jax.ShapeDtypeStruct((tiles,), jnp.int32),
            jax.ShapeDtypeStruct((2,), jnp.int32),
        ),
        in_specs=[smem, smem],
        out_specs=(smem, smem, smem),
        compiler_params=pltpu.CompilerParams(vmem_limit_bytes=MIB),
        name="plan",
    )(owners, steps)


def block_kernel(blocks, replicas, width, part_ref, *refs):
    replica_id = lax.axis_index("replica")
    *outs, sems = refs
    copies = []
    for k, (pipe, offset, start, size) in enumerate(blocks):
        column = lax.rem(replica_id + offset + replicas, replicas) * width + start
        rows = outs[k].shape[0]
        source = part_ref.at[
            pl.ds(pipe * rows, rows), :, pl.ds(pl.multiple_of(column, 128), size)
        ]
        copies.append(pltpu.make_async_copy(source, outs[k], sems.at[k]))
    for copy in copies:
        copy.start()
    for copy in copies:
        copy.wait()


def fetch_blocks(part, replicas, width, blocks, name):
    rows = part.shape[0] // RINGS
    shapes = tuple(pltpu.VMEM((rows, part.shape[1], size), part.dtype) for *_, size in blocks)
    return pl.pallas_call(
        functools.partial(block_kernel, blocks, replicas, width),
        in_specs=[pl.BlockSpec(memory_space=pl.ANY)],
        out_specs=(pl.BlockSpec(memory_space=pltpu.VMEM),) * len(blocks),
        out_shape=shapes,
        scratch_shapes=[pltpu.SemaphoreType.DMA((len(blocks),))],
        compiler_params=pltpu.CompilerParams(vmem_limit_bytes=SMALL_VMEM),
        name=name,
    )(pltpu.with_memory_space_constraint(part, pltpu.HBM))


def add_kernel(start, block_ref, arrived_ref, out_ref):
    rows, _, width = block_ref.shape
    size = arrived_ref.shape[2]
    cols = slice(start, start + size)
    rest = slice(0, start) if start else slice(size, width)
    for l in range(rows):
        out_ref[l, :, cols] = block_ref[l, :, cols] + arrived_ref[l]
        if size < width:
            out_ref[l, :, rest] = block_ref[l, :, rest]


def add_block(block, arrived, start):
    vmem = pl.BlockSpec(memory_space=pltpu.VMEM)
    return pl.pallas_call(
        functools.partial(add_kernel, start),
        in_specs=[vmem, vmem],
        out_specs=vmem,
        out_shape=pltpu.VMEM(block.shape, block.dtype),
        compiler_params=pltpu.CompilerParams(vmem_limit_bytes=SMALL_VMEM),
        name="add_block",
    )(block, pltpu.with_memory_space_constraint(arrived, pltpu.VMEM))


def pack_kernel(tile_of_ref, *refs):
    *parts, out_ref, sums_ref = refs
    rows, sub_rows, width = parts[0].shape
    half = width // 2
    for ring in range(RINGS):
        own, above, below = parts[3 * ring : 3 * ring + 3]
        for l in range(rows):
            total = own[l].astype(f32) + above[l].astype(f32) + below[l].astype(f32)
            total = total.astype(bf16)
            tile = 2 * (ring * rows + l)
            sums_ref[tile] = total[:, :half]
            sums_ref[tile + 1] = total[:, half:]
    devices_mp, capacity = out_ref.shape[:2]

    def step(m, carry):
        for c in range(capacity):
            out_ref[m, c] = sums_ref[tile_of_ref[m * capacity + c]]
        return carry

    lax.fori_loop(0, devices_mp, step, 0, unroll=4)


def pack(tile_of, parts, devices_mp, capacity):
    rows, sub_rows, width = parts[0].shape
    vmem = pl.BlockSpec(memory_space=pltpu.VMEM)
    return pl.pallas_call(
        pack_kernel,
        in_specs=[pl.BlockSpec(memory_space=pltpu.SMEM)] + [vmem] * len(parts),
        out_specs=vmem,
        out_shape=jax.ShapeDtypeStruct((devices_mp, capacity, sub_rows, width // 2), bf16),
        scratch_shapes=[pltpu.VMEM((2 * RINGS * rows, sub_rows, width // 2), bf16)],
        compiler_params=pltpu.CompilerParams(vmem_limit_bytes=VMEM_LIMIT),
        name="pack",
    )(tile_of, *parts)


def dot(a, b):
    return jnp.dot(a, b, preferred_element_type=f32)


def in_pieces(source, target, sems):
    slots, rows, _ = source.shape
    size = rows // PIECES
    return [
        pltpu.make_async_copy(
            source.at[s, pl.ds(p * size, size)], target.at[s, pl.ds(p * size, size)], sems.at[s, p]
        )
        for s in range(slots)
        for p in range(PIECES)
    ]


def prepare_kernel(
    left_hbm, right_hbm, first_hbm, second_hbm, left, left_t, right, right_t, first, second, sems
):
    pairs = ((left_hbm, left), (right_hbm, right), (first_hbm, first), (second_hbm, second))
    arrivals = [in_pieces(a, b, sems.at[k]) for k, (a, b) in enumerate(pairs)]
    for copies in arrivals:
        for copy in copies:
            copy.start()
    for k, copies in enumerate(arrivals):
        for copy in copies:
            copy.wait()
        if k < 2:
            source, target = ((left, left_t), (right, right_t))[k]
            for s in range(source.shape[0]):
                target[s] = source[s].T


def prepare(left, right, first, second):
    hbm = pl.BlockSpec(memory_space=pl.ANY)
    vmem = pl.BlockSpec(memory_space=pltpu.VMEM)
    square, wide = pltpu.VMEM(left.shape, bf16), pltpu.VMEM(left.shape, f32)
    return pl.pallas_call(
        prepare_kernel,
        in_specs=[hbm] * 4,
        out_specs=(vmem,) * 6,
        out_shape=(square, square, square, square, square, wide),
        scratch_shapes=[pltpu.SemaphoreType.DMA((4, left.shape[0], PIECES))],
        compiler_params=pltpu.CompilerParams(vmem_limit_bytes=SMALL_VMEM),
        name="prepare",
    )(*(pltpu.with_memory_space_constraint(a, pltpu.HBM) for a in (left, right, first, second)))


def tile_kernel(
    held_ref, grad, left, left_t, right, right_t, first, second,
    update, first_hbm, second_hbm, first_out, second_out, returned, sems,
):
    capacity, size, _ = left.shape
    devices_mp, _, sub_rows, _ = grad.shape
    half = size // 2
    step_value = jnp.full((8, 128), held_ref[1], jnp.int32).astype(f32)
    scale = -(1.0 - (step_value - decay_start) / decay_length)[:1, :1]
    first_fix = (1.0 / (1.0 - jnp.exp(step_value * math.log(beta_first))))[:1, :1]
    second_fix = (1.0 / (1.0 - jnp.exp(step_value * math.log(beta_second))))[:1, :1]

    def work(slots):
        projected = {
            s: dot(left_t[s], grad[:, s].reshape(size, size)).astype(bf16) for s in slots
        }
        for start in (0, half):
            cols = slice(start, start + half)
            for s in slots:
                rotated = dot(projected[s], right[s, :, cols])
                first_new = (
                    beta_first * first[s, :, cols].astype(f32) + (1.0 - beta_first) * rotated
                )
                second_new = (
                    beta_second * second[s, :, cols] + (1.0 - beta_second) * rotated * rotated
                )
                first_out[s, :, cols] = first_new.astype(bf16)
                second_out[s, :, cols] = second_new
                direction = (
                    first_new * first_fix / (jnp.sqrt(second_new * second_fix) + epsilon)
                ).astype(bf16)
                returned[s, :, cols] = dot(left[s], direction).astype(bf16)
        leave(slots)
        for s in slots:
            step = (scale * dot(returned[s], right_t[s])).astype(bf16)
            update[:, s] = step.reshape(devices_mp, sub_rows, size)

    def moments(s):
        return (
            pltpu.make_async_copy(second_out.at[s], second_hbm.at[s], sems.at[s, 0]),
            pltpu.make_async_copy(first_out.at[s], first_hbm.at[s], sems.at[s, 1]),
        )

    def leave(slots):
        for s in slots:
            for copy in moments(s):
                copy.start()

    def keep(slots):
        for s in slots:
            first_out[s] = first[s]
            second_out[s] = second[s]
            update[:, s] = jnp.zeros((devices_mp, sub_rows, size), bf16)
        leave(slots)

    for count in range(capacity + 1):

        @pl.when(held_ref[0] == count)
        def _():
            keep(range(count, capacity))
            work(range(count))

    for s in range(capacity):
        for copy in moments(s):
            copy.wait()


def tile_update(held, grads, ready):
    shape = ready[0].shape
    smem = pl.BlockSpec(memory_space=pltpu.SMEM)
    vmem = pl.BlockSpec(memory_space=pltpu.VMEM)
    hbm = pl.BlockSpec(memory_space=pl.ANY)
    return pl.pallas_call(
        tile_kernel,
        in_specs=[smem] + [vmem] * 7,
        out_specs=(vmem, hbm, hbm),
        out_shape=(
            pltpu.VMEM(grads.shape, bf16),
            jax.ShapeDtypeStruct(shape, bf16),
            jax.ShapeDtypeStruct(shape, f32),
        ),
        scratch_shapes=[
            pltpu.VMEM(shape, bf16),
            pltpu.VMEM(shape, f32),
            pltpu.VMEM(shape, bf16),
            pltpu.SemaphoreType.DMA((shape[0], 2)),
        ],
        compiler_params=pltpu.CompilerParams(vmem_limit_bytes=TILE_VMEM),
        name="tile_update",
    )(held, grads, *ready)


def place_kernel(slot_of_ref, back_ref, out_hbm, sems):
    tile_rows, sub_rows, width = out_hbm.shape
    _, _, size = back_ref.shape
    copies = [
        pltpu.make_async_copy(
            back_ref.at[slot_of_ref[t]],
            out_hbm.at[t * size // width, :, pl.ds(t * size % width, size)],
            sems.at[t],
        )
        for t in range(tile_rows * width // size)
    ]
    for copy in copies:
        copy.start()
    for copy in copies:
        copy.wait()


def place(slot_of, back, tile_rows):
    slots, sub_rows, size = back.shape
    return pl.pallas_call(
        place_kernel,
        in_specs=[
            pl.BlockSpec(memory_space=pltpu.SMEM),
            pl.BlockSpec(memory_space=pltpu.VMEM),
        ],
        out_specs=pl.BlockSpec(memory_space=pl.ANY),
        out_shape=jax.ShapeDtypeStruct((tile_rows, sub_rows, 2 * size), bf16),
        scratch_shapes=[pltpu.SemaphoreType.DMA((2 * tile_rows,))],
        compiler_params=pltpu.CompilerParams(vmem_limit_bytes=SMALL_VMEM),
        name="place",
    )(slot_of, back)


def together(*values):
    return lax.optimization_barrier(values)


def body(partials, owners, step_count, basis_left, basis_right, moment_first, moment_second):
    replicas = lax.axis_size("replica")
    devices_mp = lax.axis_size("mp")
    part, owners, steps = together(
        partials[0], jnp.swapaxes(owners, 1, 2), jnp.broadcast_to(step_count, (128,))
    )
    tile_rows, sub_rows, columns = part.shape
    capacity = basis_left.shape[2]
    width = columns // replicas
    half = width // 2
    far = replicas // 2
    up = [(i, (i + 1) % replicas) for i in range(replicas)]
    down = [(i, (i - 1) % replicas) for i in range(replicas)]

    def swap(low, high):
        return lax.ppermute(low, "replica", down), lax.ppermute(high, "replica", up)

    rings = range(RINGS)
    first = [(ring, far, start, half) for ring in rings for start in (0, half)]
    firsts = fetch_blocks(part, replicas, width, first, "first_blocks")
    moving = [swap(firsts[2 * ring], firsts[2 * ring + 1]) for ring in rings]
    _, part = together(firsts[0], part)
    rest = [
        (ring, sign * hops, 0, width)
        for hops in range(far - 1, 0, -1)
        for ring in rings
        for sign in (-1, 1)
    ]
    rest += [(ring, 0, 0, width) for ring in rings]
    blocks = list(fetch_blocks(part, replicas, width, rest, "rest_blocks"))
    owns = blocks[-RINGS:]
    state = (
        owners, steps, basis_left[0, 0], basis_right[0, 0], moment_first[0, 0], moment_second[0, 0]
    )
    for hops in range(far - 1, 0, -1):
        for ring in rings:
            above, below = moving[ring]
            low = add_block(blocks.pop(0), above, 0)
            high = add_block(blocks.pop(0), below, half if hops == far - 1 else 0)
            if ring == RINGS - 1:
                low, state = together(low, state)
            moving[ring] = swap(low, high)
        if hops == far - 1:
            owners, steps, *operands = state
            state = (make_plan(owners, steps, devices_mp, capacity), operands)
    plan, operands = state
    moving, plan, ready = together(moving, plan, prepare(*operands))
    tile_of, slot_of, held = plan
    parts = [x for ring in rings for x in (owns[ring], *moving[ring])]
    outgoing = pack(tile_of, parts, devices_mp, capacity)
    arrived = lax.all_to_all(outgoing, "mp", split_axis=0, concat_axis=0, tiled=True)
    update, first_out, second_out = tile_update(held, arrived, ready)
    back = lax.all_to_all(update, "mp", split_axis=0, concat_axis=0, tiled=True)
    back = back.reshape(devices_mp * capacity, sub_rows, half)
    slab = place(slot_of, back, tile_rows)
    return slab, first_out[None, None], second_out[None, None]


def solution(mesh):
    in_specs = (
        P("replica", None, "mp", None),
        P(),
        P(),
        P("replica", "mp", None, None, None),
        P("replica", "mp", None, None, None),
        P("replica", "mp", None, None, None),
        P("replica", "mp", None, None, None),
    )
    out_specs = (
        P(None, "mp", "replica"),
        P("replica", "mp", None, None, None),
        P("replica", "mp", None, None, None),
    )
    return jax.shard_map(body, mesh=mesh, in_specs=in_specs, out_specs=out_specs, check_vma=False)
```

```python
import functools
import math
import jax
import jax.numpy as jnp
from jax import lax
from jax.experimental import pallas as pl
from jax.experimental.pallas import tpu as pltpu
from jax.sharding import PartitionSpec as P

bf16 = jnp.bfloat16
f32 = jnp.float32
beta_first = 0.9
beta_second = 0.95
epsilon = 1e-08
decay_start = 9000.0
decay_length = 1000.0
MIB = 1024 * 1024
VMEM_LIMIT = 12 * MIB
TILE_VMEM = 24 * MIB
SMALL_VMEM = 4 * MIB
PIECES = 2
RINGS = 2


def block_copies(blocks, replicas, width, part_ref, outs, sems):
    replica_id = lax.axis_index("replica")
    copies = []
    for k, (pipe, offset, start, size) in enumerate(blocks):
        column = lax.rem(replica_id + offset + replicas, replicas) * width + start
        rows = outs[k].shape[0]
        source = part_ref.at[
            pl.ds(pipe * rows, rows), :, pl.ds(pl.multiple_of(column, 128), size)
        ]
        copies.append(pltpu.make_async_copy(source, outs[k], sems.at[k]))
    for copy in copies:
        copy.start()
    return copies


def block_kernel(blocks, replicas, width, part_ref, *refs):
    *outs, sems = refs
    for copy in block_copies(blocks, replicas, width, part_ref, outs, sems):
        copy.wait()


def plan_kernel(blocks, replicas, width, owners_ref, step_ref, part_ref, *refs):
    tile_of_ref, slot_of_ref, held_ref, *outs, sems = refs
    copies = block_copies(blocks, replicas, width, part_ref, outs, sems)
    replica_id, my_index = lax.axis_index("replica"), lax.axis_index("mp")
    _, tile_cols, tile_rows = owners_ref.shape
    devices_mp = lax.axis_size("mp")
    counts = tile_of_ref.shape[0] - devices_mp
    capacity = counts // devices_mp
    for i in range(tile_of_ref.shape[0]):
        tile_of_ref[i] = 0

    def step(l, carry):
        for j in range(tile_cols):
            owner = owners_ref[replica_id, j, l]
            rank = tile_of_ref[counts + owner]
            tile_of_ref[counts + owner] = rank + 1
            slot = owner * capacity + rank
            tile_of_ref[slot] = l * tile_cols + j
            slot_of_ref[l * tile_cols + j] = slot
        return carry

    lax.fori_loop(0, tile_rows, step, 0)
    held_ref[0] = tile_of_ref[counts + my_index]
    held_ref[1] = step_ref[0]
    for copy in copies:
        copy.wait()


def make_plan(owners, steps, part, replicas, width, blocks, devices_mp, capacity):
    rows = part.shape[0] // RINGS
    shapes = tuple(pltpu.VMEM((rows, part.shape[1], size), part.dtype) for *_, size in blocks)
    vmem = pl.BlockSpec(memory_space=pltpu.VMEM)
    tiles = owners.shape[1] * owners.shape[2]
    smem = pl.BlockSpec(memory_space=pltpu.SMEM)
    return pl.pallas_call(
        functools.partial(plan_kernel, blocks, replicas, width),
        out_shape=(
            jax.ShapeDtypeStruct((devices_mp * (capacity + 1),), jnp.int32),
            jax.ShapeDtypeStruct((tiles,), jnp.int32),
            jax.ShapeDtypeStruct((2,), jnp.int32),
        )
        + shapes,
        in_specs=[smem, smem, pl.BlockSpec(memory_space=pl.ANY)],
        out_specs=(smem, smem, smem) + (vmem,) * len(blocks),
        scratch_shapes=[pltpu.SemaphoreType.DMA((len(blocks),))],
        compiler_params=pltpu.CompilerParams(vmem_limit_bytes=MIB),
        name="plan",
    )(owners, steps, pltpu.with_memory_space_constraint(part, pltpu.HBM))


def fetch_blocks(part, replicas, width, blocks, name):
    rows = part.shape[0] // RINGS
    shapes = tuple(pltpu.VMEM((rows, part.shape[1], size), part.dtype) for *_, size in blocks)
    return pl.pallas_call(
        functools.partial(block_kernel, blocks, replicas, width),
        in_specs=[pl.BlockSpec(memory_space=pl.ANY)],
        out_specs=(pl.BlockSpec(memory_space=pltpu.VMEM),) * len(blocks),
        out_shape=shapes,
        scratch_shapes=[pltpu.SemaphoreType.DMA((len(blocks),))],
        compiler_params=pltpu.CompilerParams(vmem_limit_bytes=SMALL_VMEM),
        name=name,
    )(pltpu.with_memory_space_constraint(part, pltpu.HBM))


def add_kernel(start, block_ref, arrived_ref, out_ref):
    rows, _, width = block_ref.shape
    size = arrived_ref.shape[2]
    cols = slice(start, start + size)
    rest = slice(0, start) if start else slice(size, width)
    for l in range(rows):
        out_ref[l, :, cols] = block_ref[l, :, cols] + arrived_ref[l]
        if size < width:
            out_ref[l, :, rest] = block_ref[l, :, rest]


def add_block(block, arrived, start):
    vmem = pl.BlockSpec(memory_space=pltpu.VMEM)
    return pl.pallas_call(
        functools.partial(add_kernel, start),
        in_specs=[vmem, vmem],
        out_specs=vmem,
        out_shape=pltpu.VMEM(block.shape, block.dtype),
        compiler_params=pltpu.CompilerParams(vmem_limit_bytes=SMALL_VMEM),
        name="add_block",
    )(block, pltpu.with_memory_space_constraint(arrived, pltpu.VMEM))


def pack_kernel(tile_of_ref, *refs):
    *parts, out_ref, sums_ref = refs
    rows, sub_rows, width = parts[0].shape
    half = width // 2
    for ring in range(RINGS):
        own, above, below = parts[3 * ring : 3 * ring + 3]
        for l in range(rows):
            total = own[l].astype(f32) + above[l].astype(f32) + below[l].astype(f32)
            total = total.astype(bf16)
            tile = 2 * (ring * rows + l)
            sums_ref[tile] = total[:, :half]
            sums_ref[tile + 1] = total[:, half:]
    devices_mp, capacity = out_ref.shape[:2]

    def step(m, carry):
        for c in range(capacity):
            out_ref[m, c] = sums_ref[tile_of_ref[m * capacity + c]]
        return carry

    lax.fori_loop(0, devices_mp, step, 0, unroll=4)


def pack(tile_of, parts, devices_mp, capacity):
    rows, sub_rows, width = parts[0].shape
    vmem = pl.BlockSpec(memory_space=pltpu.VMEM)
    return pl.pallas_call(
        pack_kernel,
        in_specs=[pl.BlockSpec(memory_space=pltpu.SMEM)] + [vmem] * len(parts),
        out_specs=vmem,
        out_shape=jax.ShapeDtypeStruct((devices_mp, capacity, sub_rows, width // 2), bf16),
        scratch_shapes=[pltpu.VMEM((2 * RINGS * rows, sub_rows, width // 2), bf16)],
        compiler_params=pltpu.CompilerParams(vmem_limit_bytes=VMEM_LIMIT),
        name="pack",
    )(tile_of, *parts)


def dot(a, b):
    return jnp.dot(a, b, preferred_element_type=f32)


def in_pieces(source, target, sems):
    slots, rows, _ = source.shape
    size = rows // PIECES
    return [
        pltpu.make_async_copy(
            source.at[s, pl.ds(p * size, size)], target.at[s, pl.ds(p * size, size)], sems.at[s, p]
        )
        for s in range(slots)
        for p in range(PIECES)
    ]


def prepare_kernel(
    left_hbm, right_hbm, first_hbm, second_hbm, left, left_t, right, right_t, first, second, sems
):
    pairs = ((left_hbm, left), (right_hbm, right), (first_hbm, first), (second_hbm, second))
    arrivals = [in_pieces(a, b, sems.at[k]) for k, (a, b) in enumerate(pairs)]
    for copies in arrivals:
        for copy in copies:
            copy.start()
    for k, copies in enumerate(arrivals):
        for copy in copies:
            copy.wait()
        if k < 2:
            source, target = ((left, left_t), (right, right_t))[k]
            for s in range(source.shape[0]):
                target[s] = source[s].T


def prepare(left, right, first, second):
    hbm = pl.BlockSpec(memory_space=pl.ANY)
    vmem = pl.BlockSpec(memory_space=pltpu.VMEM)
    square, wide = pltpu.VMEM(left.shape, bf16), pltpu.VMEM(left.shape, f32)
    return pl.pallas_call(
        prepare_kernel,
        in_specs=[hbm] * 4,
        out_specs=(vmem,) * 6,
        out_shape=(square, square, square, square, square, wide),
        scratch_shapes=[pltpu.SemaphoreType.DMA((4, left.shape[0], PIECES))],
        compiler_params=pltpu.CompilerParams(vmem_limit_bytes=SMALL_VMEM),
        name="prepare",
    )(*(pltpu.with_memory_space_constraint(a, pltpu.HBM) for a in (left, right, first, second)))


def tile_kernel(
    held_ref, grad, left, left_t, right, right_t, first, second,
    update, first_hbm, second_hbm, first_out, second_out, returned, sems,
):
    capacity, size, _ = left.shape
    devices_mp, _, sub_rows, _ = grad.shape
    half = size // 2
    step_value = jnp.full((8, 128), held_ref[1], jnp.int32).astype(f32)
    scale = -(1.0 - (step_value - decay_start) / decay_length)[:1, :1]
    first_fix = (1.0 / (1.0 - jnp.exp(step_value * math.log(beta_first))))[:1, :1]
    second_fix = (1.0 / (1.0 - jnp.exp(step_value * math.log(beta_second))))[:1, :1]

    def work(slots):
        projected = {
            s: dot(left_t[s], grad[:, s].reshape(size, size)).astype(bf16) for s in slots
        }
        for start in (0, half):
            cols = slice(start, start + half)
            for s in slots:
                rotated = dot(projected[s], right[s, :, cols])
                first_new = (
                    beta_first * first[s, :, cols].astype(f32) + (1.0 - beta_first) * rotated
                )
                second_new = (
                    beta_second * second[s, :, cols] + (1.0 - beta_second) * rotated * rotated
                )
                first_out[s, :, cols] = first_new.astype(bf16)
                second_out[s, :, cols] = second_new
                direction = (
                    first_new * first_fix / (jnp.sqrt(second_new * second_fix) + epsilon)
                ).astype(bf16)
                returned[s, :, cols] = dot(left[s], direction).astype(bf16)
        leave(slots)
        for s in slots:
            step = (scale * dot(returned[s], right_t[s])).astype(bf16)
            update[:, s] = step.reshape(devices_mp, sub_rows, size)

    def moments(s):
        return (
            pltpu.make_async_copy(second_out.at[s], second_hbm.at[s], sems.at[s, 0]),
            pltpu.make_async_copy(first_out.at[s], first_hbm.at[s], sems.at[s, 1]),
        )

    def leave(slots):
        for s in slots:
            for copy in moments(s):
                copy.start()

    def keep(slots):
        for s in slots:
            first_out[s] = first[s]
            second_out[s] = second[s]
            update[:, s] = jnp.zeros((devices_mp, sub_rows, size), bf16)
        leave(slots)

    for count in range(capacity + 1):

        @pl.when(held_ref[0] == count)
        def _():
            keep(range(count, capacity))
            work(range(count))

    for s in range(capacity):
        for copy in moments(s):
            copy.wait()


def tile_update(held, grads, ready):
    shape = ready[0].shape
    smem = pl.BlockSpec(memory_space=pltpu.SMEM)
    vmem = pl.BlockSpec(memory_space=pltpu.VMEM)
    hbm = pl.BlockSpec(memory_space=pl.ANY)
    return pl.pallas_call(
        tile_kernel,
        in_specs=[smem] + [vmem] * 7,
        out_specs=(vmem, hbm, hbm),
        out_shape=(
            pltpu.VMEM(grads.shape, bf16),
            jax.ShapeDtypeStruct(shape, bf16),
            jax.ShapeDtypeStruct(shape, f32),
        ),
        scratch_shapes=[
            pltpu.VMEM(shape, bf16),
            pltpu.VMEM(shape, f32),
            pltpu.VMEM(shape, bf16),
            pltpu.SemaphoreType.DMA((shape[0], 2)),
        ],
        compiler_params=pltpu.CompilerParams(vmem_limit_bytes=TILE_VMEM),
        name="tile_update",
    )(held, grads, *ready)


def place_kernel(slot_of_ref, back_ref, out_hbm, sems):
    tile_rows, sub_rows, width = out_hbm.shape
    _, _, size = back_ref.shape
    copies = [
        pltpu.make_async_copy(
            back_ref.at[slot_of_ref[t]],
            out_hbm.at[t * size // width, :, pl.ds(t * size % width, size)],
            sems.at[t],
        )
        for t in range(tile_rows * width // size)
    ]
    for copy in copies:
        copy.start()
    for copy in copies:
        copy.wait()


def place(slot_of, back, tile_rows):
    slots, sub_rows, size = back.shape
    return pl.pallas_call(
        place_kernel,
        in_specs=[
            pl.BlockSpec(memory_space=pltpu.SMEM),
            pl.BlockSpec(memory_space=pltpu.VMEM),
        ],
        out_specs=pl.BlockSpec(memory_space=pl.ANY),
        out_shape=jax.ShapeDtypeStruct((tile_rows, sub_rows, 2 * size), bf16),
        scratch_shapes=[pltpu.SemaphoreType.DMA((2 * tile_rows,))],
        compiler_params=pltpu.CompilerParams(vmem_limit_bytes=SMALL_VMEM),
        name="place",
    )(slot_of, back)


def together(*values):
    return lax.optimization_barrier(values)


def body(partials, owners, step_count, basis_left, basis_right, moment_first, moment_second):
    replicas = lax.axis_size("replica")
    devices_mp = lax.axis_size("mp")
    part, owners, steps = together(
        partials[0], jnp.swapaxes(owners, 1, 2), jnp.broadcast_to(step_count, (128,))
    )
    tile_rows, sub_rows, columns = part.shape
    capacity = basis_left.shape[2]
    width = columns // replicas
    half = width // 2
    far = replicas // 2
    up = [(i, (i + 1) % replicas) for i in range(replicas)]
    down = [(i, (i - 1) % replicas) for i in range(replicas)]

    def swap(low, high):
        return lax.ppermute(low, "replica", down), lax.ppermute(high, "replica", up)

    rings = range(RINGS)
    first = [(ring, far, start, half) for ring in rings for start in (0, half)]
    firsts = fetch_blocks(part, replicas, width, first, "first_blocks")
    moving = [swap(firsts[2 * ring], firsts[2 * ring + 1]) for ring in rings]
    _, part = together(firsts[0], part)
    rest = [
        (ring, sign * hops, 0, width)
        for hops in range(far - 1, 0, -1)
        for ring in rings
        for sign in (-1, 1)
    ]
    blocks = list(fetch_blocks(part, replicas, width, rest, "rest_blocks"))
    state = (
        owners, steps, basis_left[0, 0], basis_right[0, 0], moment_first[0, 0], moment_second[0, 0]
    )
    for hops in range(far - 1, 0, -1):
        for ring in rings:
            above, below = moving[ring]
            low = add_block(blocks.pop(0), above, 0)
            high = add_block(blocks.pop(0), below, half if hops == far - 1 else 0)
            if ring == RINGS - 1:
                low, state = together(low, state)
            moving[ring] = swap(low, high)
        if hops == far - 1:
            owners, steps, *operands = state
            late = [(ring, 0, 0, width) for ring in rings]
            *plan, = make_plan(owners, steps, part, replicas, width, late, devices_mp, capacity)
            blocks += plan[3:-RINGS]
            owns = plan[-RINGS:]
            state = (tuple(plan[:3]), operands)
    plan, operands = state
    moving, plan, ready = together(moving, plan, prepare(*operands))
    tile_of, slot_of, held = plan
    parts = [x for ring in rings for x in (owns[ring], *moving[ring])]
    outgoing = pack(tile_of, parts, devices_mp, capacity)
    arrived = lax.all_to_all(outgoing, "mp", split_axis=0, concat_axis=0, tiled=True)
    update, first_out, second_out = tile_update(held, arrived, ready)
    back = lax.all_to_all(update, "mp", split_axis=0, concat_axis=0, tiled=True)
    back = back.reshape(devices_mp * capacity, sub_rows, half)
    slab = place(slot_of, back, tile_rows)
    return slab, first_out[None, None], second_out[None, None]


def solution(mesh):
    in_specs = (
        P("replica", None, "mp", None),
        P(),
        P(),
        P("replica", "mp", None, None, None),
        P("replica", "mp", None, None, None),
        P("replica", "mp", None, None, None),
        P("replica", "mp", None, None, None),
    )
    out_specs = (
        P(None, "mp", "replica"),
        P("replica", "mp", None, None, None),
        P("replica", "mp", None, None, None),
    )
    return jax.shard_map(body, mesh=mesh, in_specs=in_specs, out_specs=out_specs, check_vma=False)
```
